32 devices in a mesh: groups: 2 (over x), clu: 16 (over z, y, core).
Axes of the slice: x: 2, y: 2, z: 4, core: 2. Of those that a mesh axis runs over, the one named last changes fastest.
Arguments:
- values: bfloat16 [32768, 64], P(('groups', 'clu')), parts along dimension 0, may hold values from -6 to 6
- basis: bfloat16 [512, 64, 64], P(('groups', 'clu')), parts along dimension 0, may hold values from -0.75 to 0.75
- transfer: bfloat16 [512, 64, 64], P(('groups', 'clu')), parts along dimension 0, may hold values from -0.25 to 0.25
- near_list: int32 [512, 8], P(('groups', 'clu')), parts along dimension 0, may hold values from 0 to 15
- near_blocks: bfloat16 [512, 8, 64, 64], P(('groups', 'clu')), parts along dimension 0, may hold values from -0.1875 to 0.1875
- far_list: int32 [512, 8], P(('groups', 'clu')), parts along dimension 0, may hold values from 0 to 15
- far_blocks: bfloat16 [512, 8, 64, 64], P(('groups', 'clu')), parts along dimension 0, may hold values from -0.1875 to 0.1875
- near_plan: int32 [32, 2, 24], P(('groups', 'clu')), parts along dimension 0, may hold values from -1 to 15, as said below
- near_remote: bfloat16 [32, 24, 64, 64], P(('groups', 'clu')), parts along dimension 0, may hold values from -0.1875 to 0.1875
- far_plan: int32 [32, 2, 72], P(('groups', 'clu')), parts along dimension 0, may hold values from -1 to 15, as said below
- far_remote: bfloat16 [32, 72, 64, 64], P(('groups', 'clu')), parts along dimension 0, may hold values from -0.1875 to 0.1875
- parent_plan: int32 [32, 2, 32], P(('groups', 'clu')), parts along dimension 0, may hold values from -1 to 1, as said below
- parent_remote: bfloat16 [32, 32, 64, 64], P(('groups', 'clu')), parts along dimension 0, may hold values from -0.1875 to 0.1875
Outputs:
- first_product: bfloat16 [32768, 64], P(('groups', 'clu')), parts along dimension 0
- second_product: bfloat16 [32768, 64], P(('groups', 'clu')), parts along dimension 0
The draws below stay inside these ranges and needn't reach their ends.
There are 2 independent parts, one for each index of `groups`. The reference program is written for one: setup_inputs(seed, part) draws one part's arguments, and reference() takes and returns one part's arrays. A program takes and returns all parts, laid end to end along the dimension named above; each array names one. Nothing has to cross between parts.
Inputs may be any that keep to these rules, and one draw needn't show every extreme that they name: `far_plan`: neighbour plan of capacity 6 as described in the reference program: in each group of 6 slots the live ones come first; slots whose source device lies outside the mesh are empty; for every target device some neighbour fills all 6 slots. `near_plan`: neighbour plan of capacity 2 as described in the reference program, live slots first in each group, slots whose source device lies outside the mesh empty; for every target device some neighbour fills all 2 slots. `parent_plan`: plan of capacity 2 over parents as described in the reference program, live slots first in each group; for every target device one source device fills all 2 slots.
All inputs are finite; a program needn't handle non-finite values.
Results may differ from the reference program's by a relative error of at most 0.0071.
Values may be sent and summed in bfloat16 or wider, within the bound.
No kernel may reach another device: no remote copies, remote signals or barrier semaphores. Data moves between devices by JAX's collectives and lax.ppermute only.
A program may use at most 128 MiB of HBM per device.

```python
import jax
import jax.numpy as jnp
from jax import lax

LEAF = 64
RANK = 64
NRHS = 64
LEAF_DEV = 16
NNL = 8
NFL = 8
HOPS = 6
CAP0 = 6
CAPN = 2
CAP1 = 2
PAR_DEV = 2
LEAVES = 256
POINTS = 16384
N_CLU = 16


def slot_plan(key, slot_cap, source_range, target_range):
    subkeys = jax.random.split(key, 4)
    counts = jax.random.randint(subkeys[0], (N_CLU, N_CLU), 0, slot_cap + 1)
    crowded = jax.random.randint(subkeys[1], (N_CLU, 1), 0, 4) == 0
    counts = jnp.where(crowded, slot_cap, counts)
    row_ids = jnp.arange(N_CLU)[:, None]
    col_ids = jnp.arange(N_CLU)[None, :]
    counts = jnp.where(col_ids == (row_ids + 1) % N_CLU, slot_cap, counts)
    filled = jnp.arange(slot_cap)[None, None, :] < counts[:, :, None]
    source_leaf = jnp.where(filled, jax.random.randint(subkeys[2], (N_CLU, N_CLU, slot_cap), 0, source_range), -1)
    target_leaf = jnp.where(filled, jax.random.randint(subkeys[3], (N_CLU, N_CLU, slot_cap), 0, target_range), -1)
    stacked = jnp.stack([source_leaf.reshape(N_CLU, N_CLU * slot_cap), target_leaf.reshape(N_CLU, N_CLU * slot_cap)], axis=1)
    return stacked.astype(jnp.int32)


def neighbour_plan(key, slot_cap, source_range, target_range):
    subkeys = jax.random.split(key, 4)
    offsets = jnp.concatenate([jnp.arange(-HOPS, 0), jnp.arange(1, HOPS + 1)])
    sources = jnp.arange(N_CLU)[:, None] + offsets[None, :]
    inside = (sources >= 0) & (sources < N_CLU)
    counts = jax.random.randint(subkeys[0], (N_CLU, 2 * HOPS), (slot_cap + 1) // 2, slot_cap + 1)
    closest = (offsets[None, :] == 1) | (offsets[None, :] == -1)
    counts = jnp.where(closest, slot_cap, counts)
    counts = jnp.where(inside, counts, 0)
    filled = jnp.arange(slot_cap)[None, None, :] < counts[:, :, None]
    source_leaf = jnp.where(filled, jax.random.randint(subkeys[2], (N_CLU, 2 * HOPS, slot_cap), 0, source_range), -1)
    target_leaf = jnp.where(filled, jax.random.randint(subkeys[3], (N_CLU, 2 * HOPS, slot_cap), 0, target_range), -1)
    stacked = jnp.stack([source_leaf.reshape(N_CLU, 2 * HOPS * slot_cap), target_leaf.reshape(N_CLU, 2 * HOPS * slot_cap)], axis=1)
    return stacked.astype(jnp.int32)


def draw_near_plan(key, part):
    key = jax.random.fold_in(key, 11)
    return neighbour_plan(key, CAPN, LEAF_DEV, LEAF_DEV)


def draw_far_plan(key, part):
    key = jax.random.fold_in(key, 12)
    return neighbour_plan(key, CAP0, LEAF_DEV, LEAF_DEV)


def draw_parent_plan(key, part):
    key = jax.random.fold_in(key, 13)
    return slot_plan(key, CAP1, PAR_DEV, PAR_DEV)


def touch_ends(drawn, stream_key, least, largest):
    longest = drawn.shape.index(max(drawn.shape))
    spots = []
    for shift in (0, 1):
        where = [jax.random.randint(jax.random.fold_in(stream_key, axis), (), 0, length) for axis, length in enumerate(drawn.shape)]
        where[longest] = (where[longest] + shift) % drawn.shape[longest]
        spots.append(tuple(where))
    return drawn.at[spots[0]].set(least).at[spots[1]].set(largest)


def levels(rng, dims, shards, least, largest):
    def one(position, parts):
        draws = jax.random.uniform(jax.random.fold_in(jax.random.fold_in(rng, 6), position), (parts,), jnp.float32, least / len(shards), largest / len(shards))
        return jnp.repeat(jnp.exp(draws), dims[position] // parts).reshape((-1,) + (1,) * (len(dims) - position - 1))

    factor_of = one(*shards[0])
    for cut in shards[1:]:
        factor_of = factor_of * one(*cut)
    return factor_of


def scatter_about(key, shape, scale, bound, cuts=(), kind=jnp.bfloat16):
    entries = scale * jax.random.normal(key, shape, jnp.float32)
    if cuts:
        entries = entries * levels(key, shape, cuts, -0.22, 0.18)
    return jnp.clip(entries, -bound, bound).astype(kind)


def setup_inputs(seed: int = 0, part: int = 0) -> dict:
    keys = jax.random.split(jax.random.key(seed), 14)
    own_keys = jax.random.split(jax.random.fold_in(keys[13], part), 14)
    values = scatter_about(own_keys[0], (POINTS, NRHS), 1.0, 6.0, ((0, 16),))
    basis = scatter_about(own_keys[1], (LEAVES, LEAF, RANK), LEAF ** -0.5, 0.75, ((0, 16),))
    transfer = scatter_about(own_keys[2], (LEAVES, RANK, RANK), (RANK * 8) ** -0.5, 0.25, ((0, 16),))
    near_list = touch_ends(jax.random.randint(own_keys[3], (LEAVES, NNL), 0, LEAF_DEV), jax.random.fold_in(own_keys[3], 1), 0, LEAF_DEV - 1).astype(jnp.int32)
    near_blocks = scatter_about(own_keys[4], (LEAVES, NNL, LEAF, LEAF), (LEAF * (NNL + 8)) ** -0.5, 0.1875, ((0, 16),))
    far_list = touch_ends(jax.random.randint(own_keys[5], (LEAVES, NFL), 0, LEAF_DEV), jax.random.fold_in(own_keys[5], 1), 0, LEAF_DEV - 1).astype(jnp.int32)
    far_blocks = scatter_about(own_keys[6], (LEAVES, NFL, RANK, RANK), (RANK * (NFL + 8)) ** -0.5, 0.1875, ((0, 16),))
    near_plan = draw_near_plan(jax.random.fold_in(jax.random.fold_in(keys[13], part), 71), part)
    near_remote = scatter_about(own_keys[8], (N_CLU, 2 * HOPS * CAPN, LEAF, LEAF), (LEAF * (NNL + 8)) ** -0.5, 0.1875, ((0, 16),))
    far_plan = draw_far_plan(jax.random.fold_in(jax.random.fold_in(keys[13], part), 71), part)
    far_remote = scatter_about(own_keys[10], (N_CLU, 2 * HOPS * CAP0, RANK, RANK), (RANK * (NFL + 8)) ** -0.5, 0.1875, ((0, 16),))
    parent_plan = draw_parent_plan(jax.random.fold_in(jax.random.fold_in(keys[13], part), 71), part)
    parent_remote = scatter_about(own_keys[12], (N_CLU, N_CLU * CAP1, RANK, RANK), (RANK * N_CLU * CAP1 // PAR_DEV) ** -0.5, 0.1875, ((0, 16),))
    return dict(values=values, basis=basis, transfer=transfer, near_list=near_list, near_blocks=near_blocks, far_list=far_list, far_blocks=far_blocks, near_plan=near_plan, near_remote=near_remote, far_plan=far_plan, far_remote=far_remote, parent_plan=parent_plan, parent_remote=parent_remote)


def lift(values, basis, transfer):
    leaf_rows = values.reshape(-1, LEAF, NRHS)
    coarse = jnp.einsum('lpr,lpn->lrn', basis.astype(jnp.float32), leaf_rows.astype(jnp.float32)).astype(jnp.bfloat16)
    parent_rows = jnp.einsum('lab,lan->lbn', transfer.astype(jnp.float32), coarse.astype(jnp.float32))
    parent_rows = parent_rows.reshape(-1, 8, RANK, NRHS).sum(axis=1).astype(jnp.bfloat16)
    return leaf_rows, coarse, parent_rows


def neighbour_offsets():
    return jnp.concatenate([jnp.arange(-HOPS, 0, dtype=jnp.int32), jnp.arange(1, HOPS + 1, dtype=jnp.int32)]).astype(jnp.int32)


def plan_terms(plan, blocks, source, width_out, owners):
    source_leaf = plan[0]
    target_leaf = plan[1]
    per_device = source.shape[0] // N_CLU
    lookup = (jnp.clip(owners, 0, N_CLU - 1) * per_device + jnp.maximum(source_leaf, 0)).astype(jnp.int32)
    fetched = source[lookup].astype(jnp.float32)
    partial_terms = jnp.einsum('sab,sbn->san', blocks.astype(jnp.float32), fetched)
    select = (target_leaf[None, :] == jnp.arange(width_out, dtype=jnp.int32)[:, None]).astype(jnp.float32)
    return jnp.einsum('ls,san->lan', select, partial_terms, precision=lax.Precision.HIGHEST)


def product(values, basis, transfer, near_list, near_blocks, far_list, far_blocks, near_plan, near_remote, far_plan, far_remote, parent_plan, parent_remote):
    leaf_rows, coarse, parent_rows = lift(values, basis, transfer)
    offsets = neighbour_offsets()
    far_shift = jnp.repeat(offsets, CAP0).astype(jnp.int32)
    near_shift = jnp.repeat(offsets, CAPN).astype(jnp.int32)
    parent_owner = (jnp.arange(N_CLU * CAP1, dtype=jnp.int32) // CAP1).astype(jnp.int32)

    def per_device(packed):
        device, basis_here, transfer_here, near_here, near_mats, far_here, far_mats, near_slots, near_rmats, far_slots, far_rmats, parent_slots, parent_rmats = packed
        offset = device * LEAF_DEV
        coarse_here = lax.dynamic_slice_in_dim(coarse, offset, LEAF_DEV, 0)
        rows_here = lax.dynamic_slice_in_dim(leaf_rows, offset, LEAF_DEV, 0)
        local_far = jnp.einsum('lkab,lkbn->lan', far_mats.astype(jnp.float32), coarse_here[far_here].astype(jnp.float32))
        remote_far = plan_terms(far_slots, far_rmats, coarse, LEAF_DEV, device + far_shift)
        parent_sum = plan_terms(parent_slots, parent_rmats, parent_rows, PAR_DEV, parent_owner).astype(jnp.bfloat16)
        downward = jnp.einsum('lab,lbn->lan', transfer_here.astype(jnp.float32), jnp.repeat(parent_sum, 8, axis=0).astype(jnp.float32))
        summed = (local_far + remote_far + downward).astype(jnp.bfloat16)
        local_near = jnp.einsum('lkpq,lkqn->lpn', near_mats.astype(jnp.float32), rows_here[near_here].astype(jnp.float32))
        remote_near = plan_terms(near_slots, near_rmats, leaf_rows, LEAF_DEV, device + near_shift)
        result = jnp.einsum('lpr,lrn->lpn', basis_here.astype(jnp.float32), summed.astype(jnp.float32)) + local_near + remote_near
        return result.astype(jnp.bfloat16)

    packed = (jnp.arange(N_CLU, dtype=jnp.int32),
              basis.reshape(N_CLU, LEAF_DEV, LEAF, RANK),
              transfer.reshape(N_CLU, LEAF_DEV, RANK, RANK),
              near_list.reshape(N_CLU, LEAF_DEV, NNL),
              near_blocks.reshape(N_CLU, LEAF_DEV, NNL, LEAF, LEAF),
              far_list.reshape(N_CLU, LEAF_DEV, NFL),
              far_blocks.reshape(N_CLU, LEAF_DEV, NFL, RANK, RANK),
              near_plan, near_remote, far_plan, far_remote, parent_plan, parent_remote)
    output = lax.map(per_device, packed)
    return output.reshape(-1, NRHS)


def reference(values, basis, transfer, near_list, near_blocks, far_list, far_blocks, near_plan, near_remote, far_plan, far_remote, parent_plan, parent_remote):
    tables = (basis, transfer, near_list, near_blocks, far_list, far_blocks, near_plan, near_remote, far_plan, far_remote, parent_plan, parent_remote)
    first_product = product(values, *tables)
    second_product = product(first_product, *tables)
    return (first_product, second_product)
```

```python
import jax
import jax.numpy as jnp
from jax import lax
from jax.experimental import pallas as pl
from jax.experimental.pallas import tpu as pltpu
from jax.sharding import PartitionSpec as P


HOPS = 6
CAP0 = 6
CAPN = 2
FAN = 8
REACH = (HOPS + 1) // 2
OFFSETS = 2 * HOPS
FAR_TILES = CAP0 // 2
PAIR_TILES = (CAP0 + CAPN) // 2
F32 = jnp.float32
BF16 = jnp.bfloat16
VMEM = pl.BlockSpec(memory_space=pltpu.VMEM)
SMEM = pl.BlockSpec(memory_space=pltpu.SMEM)
PARAMS = pltpu.CompilerParams(vmem_limit_bytes=24 * 1024 * 1024)


def nn(a, b):
    return jnp.dot(a, b, preferred_element_type=F32)


def nt(a, b):
    return lax.dot_general(a, b, (((1,), (1,)), ((), ())), preferred_element_type=F32)


def beside(a, b):
    return jnp.concatenate([a, b], axis=1)


def chip_groups(devices):
    return [[2 * c, 2 * c + 1] for c in range(devices // 2)]


def outward(devices, by):
    chips = devices // 2
    up = [(2 * c, 2 * (c + by)) for c in range(chips) if c + by < chips]
    return up + [(2 * c + 1, 2 * (c - by) + 1) for c in range(chips) if c - by >= 0]


def asking(devices, by):
    chips = devices // 2
    down = [(2 * c + 1, 2 * (c - by)) for c in range(chips) if c - by >= 0]
    return down + [(2 * c, 2 * (c + by) + 1) for c in range(chips) if c + by < chips]


def offset_index(off):
    where = off + HOPS - jnp.where(off > 0, 1, 0)
    return jnp.clip(where, 0, OFFSETS - 1)


def lift_tiles(tiles, basis, transfer, own, up):
    count = len(tiles)
    sums = []
    for i, tile in enumerate(tiles):
        width = basis.shape[1]
        c0 = nn(tile[:, :width], basis[2 * i])
        c1 = nn(tile[:, width:], basis[2 * i + 1])
        coarse = beside(c0, c1).astype(BF16)
        own[i] = coarse
        own[count + i] = tile
        part = nn(coarse[:, :width], transfer[2 * i]) + nn(coarse[:, width:], transfer[2 * i + 1])
        if i % (FAN // 2) == 0:
            sums.append(part)
        else:
            sums[-1] = sums[-1] + part
    parents = beside(*sums).astype(BF16)
    for c in range(up.shape[0]):
        up[c] = parents


def lift_kernel(values, basis, transfer, own, up):
    tiles = [values[:, 128 * i : 128 * (i + 1)] for i in range(values.shape[1] // 128)]
    lift_tiles(tiles, basis, transfer, own, up)


def turn_tables(both, table):
    cores, count = both.shape[0], both.shape[1]
    for core in range(cores):
        for i in range(count):
            tile = both[core, i]
            table[0, core * count + i] = tile
            table[1, core * count + i] = beside(tile[:, 64:], tile[:, :64])


def at_left(table, base, leaf):
    return table[leaf % 2, base + leaf // 2]


def at_right(table, base, leaf):
    return table[1 - leaf % 2, base + leaf // 2]


def pair_of(table, base, first, second, left):
    return jnp.where(left, at_left(table, base, first), at_right(table, base, second))


def left_mask():
    return lax.broadcasted_iota(jnp.int32, (64, 128), 1) < 64


def pack_kernel(core_ref, *refs):
    asks = refs[:REACH]
    both = refs[REACH]
    outs = refs[REACH + 1 : REACH + 1 + REACH]
    table = refs[-1]
    core = core_ref[0]
    turn_tables(both, table)
    left = left_mask()
    half = both.shape[1]
    for step in range(REACH):
        ask, out = asks[step], outs[step]
        toward = jnp.where(core == 0, -2 * (step + 1), 2 * (step + 1))
        for target in range(2):
            for source in range(2):
                order = offset_index(toward + source - target)
                for i in range(PAIR_TILES):
                    if i < FAR_TILES:
                        at = order * CAP0 + 2 * i
                        base = source * half
                    else:
                        at = OFFSETS * CAP0 + order * CAPN + 2 * (i - FAR_TILES)
                        base = source * half + half // 2
                    first = jnp.maximum(ask[target, at], 0)
                    second = jnp.maximum(ask[target, at + 1], 0)
                    out[(target * 2 + source) * PAIR_TILES + i] = pair_of(
                        table, base, first, second, left
                    )


def local_kernel(
    core_ref, far_list, near_list, far_plan, near_plan, both, far_blocks, near_blocks, far_remote,
    near_remote, far_out, near_out, table
):
    core = core_ref[0]
    turn_tables(both, table)
    left = left_mask()
    half = both.shape[1]
    leaves = far_blocks.shape[0]

    def one_leaf(leaf, carry):
        for listed, blocks, out, kind in (
            (far_list, far_blocks, far_out, 0),
            (near_list, near_blocks, near_out, 1),
        ):
            base = core * half + kind * (half // 2)
            total = jnp.zeros((64, 64), F32)
            for k in range(0, blocks.shape[1], 2):
                x = pair_of(table, base, listed[k, leaf], listed[k + 1, leaf], left)
                total = total + nt(x, beside(blocks[leaf, k], blocks[leaf, k + 1]))
            out[leaf] = total
        return carry

    lax.fori_loop(0, leaves, one_leaf, 0)
    order = jnp.where(core == 0, HOPS, HOPS - 1)
    for plan, blocks, out, kind, cap in (
        (far_plan, far_remote, far_out, 0, CAP0),
        (near_plan, near_remote, near_out, 1, CAPN),
    ):
        base = (1 - core) * half + kind * (half // 2)
        out[leaves] = jnp.zeros((64, 64), F32)
        for c in range(cap):
            slot = order * cap + c
            target = plan[0, 1, slot]
            where = jnp.where(target < 0, leaves, target)
            x = at_left(table, base, jnp.maximum(plan[0, 0, slot], 0))[:, :64]
            out[where] = out[where] + nt(x, blocks[slot])


def combine(
    core_ref, far_plan, near_plan, parent_plan, arrived, parents, far_in, near_in, far_remote,
    near_remote, parent_remote, basis, transfer, far_acc, near_acc
):
    core = core_ref[0]
    leaves = basis.shape[0]
    far_acc[...] = far_in[...]
    near_acc[...] = near_in[...]
    for step in range(REACH):
        for side in range(2):
            for source in range(2):
                off = (2 * side - 1) * 2 * (step + 1) + source - core
                inside = jnp.logical_and(off >= -HOPS, off <= HOPS)
                order = offset_index(off)
                for i in range(PAIR_TILES):
                    tile = arrived[step][side, (core * 2 + source) * PAIR_TILES + i]
                    if i < FAR_TILES:
                        plan, blocks, acc = far_plan, far_remote, far_acc
                        slot = order * CAP0 + 2 * i
                    else:
                        plan, blocks, acc = near_plan, near_remote, near_acc
                        slot = order * CAPN + 2 * (i - FAR_TILES)
                    for c in range(2):
                        target = plan[0, 1, slot + c]
                        live = jnp.logical_and(inside, target >= 0)
                        where = jnp.where(live, target, leaves)
                        x = tile[:, 64 * c : 64 * (c + 1)]
                        acc[where] = acc[where] + nt(x, blocks[slot + c])

    chips = parents.shape[1]
    left = left_mask()

    def one_chip(chip, total):
        for member in range(2):
            tile = parents[member, chip]
            turned = beside(tile[:, 64:], tile[:, :64])
            slot = (2 * chip + member) * 2
            s0, s1 = parent_plan[0, 0, slot], parent_plan[0, 0, slot + 1]
            t0, t1 = parent_plan[0, 1, slot], parent_plan[0, 1, slot + 1]
            x0 = jnp.where(s0 > 0, turned, tile)
            x1 = jnp.where(s1 == 0, turned, tile)
            zero = jnp.zeros_like(tile)
            rows = []
            for p in range(2):
                x = jnp.where(left, jnp.where(t0 == p, x0, zero), jnp.where(t1 == p, x1, zero))
                rows.append(x)
            weights = beside(parent_remote[slot], parent_remote[slot + 1])
            total = total + nt(jnp.concatenate(rows, axis=0), weights)
        return total

    total = jnp.zeros((128, 64), F32)
    if chips <= 8:
        for chip in range(chips):
            total = one_chip(chip, total)
    else:
        total = lax.fori_loop(0, chips, one_chip, total)
    parent_sum = total.astype(BF16)

    tiles = []
    for i in range(leaves // 2):
        halves = []
        for leaf in (2 * i, 2 * i + 1):
            p = leaf // FAN
            down = nt(parent_sum[64 * p : 64 * (p + 1)], transfer[leaf])
            summed = (far_acc[leaf] + down).astype(BF16)
            halves.append(nt(summed, basis[leaf]) + near_acc[leaf])
        tiles.append(beside(*halves).astype(BF16))
    return tiles


def split_refs(refs):
    core_ref, far_plan, near_plan, parent_plan = refs[:4]
    arrived = refs[4 : 4 + REACH]
    return (core_ref, far_plan, near_plan, parent_plan, arrived) + tuple(refs[4 + REACH :])


def middle_kernel(*refs):
    out, own, up, far_acc, near_acc = refs[-5:]
    args = split_refs(refs[:-5])
    basis, transfer = refs[-7], refs[-6]
    tiles = combine(*args, far_acc, near_acc)
    for i, tile in enumerate(tiles):
        out[:, 128 * i : 128 * (i + 1)] = tile
    lift_tiles(tiles, basis, transfer, own, up)


def last_kernel(*refs):
    out, far_acc, near_acc = refs[-3:]
    tiles = combine(*split_refs(refs[:-3]), far_acc, near_acc)
    for i, tile in enumerate(tiles):
        out[:, 128 * i : 128 * (i + 1)] = tile


def call(kernel, kinds, outs, scratch, args, flops):
    size = sum(a.size * a.dtype.itemsize for a in args)
    return pl.pallas_call(
        kernel,
        out_shape=outs,
        in_specs=[SMEM if k == "s" else VMEM for k in kinds],
        out_specs=jax.tree.map(lambda _: VMEM, outs),
        scratch_shapes=scratch,
        compiler_params=PARAMS,
        cost_estimate=pl.CostEstimate(flops=flops, bytes_accessed=size, transcendentals=0),
    )(*args)


def on_device(
    values,
    basis,
    transfer,
    near_list,
    near_blocks,
    far_list,
    far_blocks,
    near_plan,
    near_remote,
    far_plan,
    far_remote,
    parent_plan,
    parent_remote,
):
    devices = lax.axis_size("clu")
    chips = devices // 2
    groups = chip_groups(devices)
    leaves = basis.shape[0]
    core = (lax.axis_index("clu") % 2).astype(jnp.int32).reshape(1)
    near_remote, far_remote, parent_remote = near_remote[0], far_remote[0], parent_remote[0]
    far_list, near_list = far_list.T, near_list.T
    same_core = [[2 * c + k for c in range(chips)] for k in range(2)]

    asks = jnp.concatenate([far_plan[0, 0], near_plan[0, 0]])
    asks = jnp.pad(asks, (0, 128 - asks.shape[0]))[None]
    asks = lax.all_gather(asks, "clu", tiled=True, axis_index_groups=groups)
    asked = [lax.ppermute(asks, "clu", asking(devices, d + 1)) for d in range(REACH)]

    shape = jax.ShapeDtypeStruct
    own_shape = shape((leaves, 64, 128), BF16)
    up_shape = shape((chips, 64, 128), BF16)
    out_shape = shape((64, values.shape[0]), BF16)
    acc_shape = shape((leaves + 1, 64, 64), F32)
    acc_scratch = [pltpu.VMEM((leaves + 1, 64, 64), F32)] * 2
    table_scratch = [pltpu.VMEM((2, 2 * leaves, 64, 128), BF16)]
    message = shape((4 * PAIR_TILES, 64, 128), BF16)
    block = 2 * 64**3

    def exchange(own, up):
        both = lax.all_gather(own, "clu", axis_index_groups=groups)
        packed = call(
            pack_kernel, "s" * (1 + REACH) + "v", [message] * REACH, table_scratch,
            (core, *asked, both), 1000,
        )
        moved = [
            lax.ppermute(m, "clu", outward(devices, d + 1)) for d, m in enumerate(packed)
        ]
        parents = lax.all_to_all(
            up, "clu", 0, 0, tiled=True, axis_index_groups=same_core
        )
        parents = lax.all_gather(parents, "clu", axis_index_groups=groups)
        far_acc, near_acc = call(
            local_kernel, "sssssvvvvv", [acc_shape] * 2, table_scratch,
            (core, far_list, near_list, far_plan, near_plan, both, far_blocks, near_blocks,
             far_remote, near_remote),
            2 * 8 * leaves * block,
        )
        arrived = [lax.all_gather(m, "clu", axis_index_groups=groups) for m in moved]
        return (
            core, far_plan, near_plan, parent_plan, *arrived, parents, far_acc, near_acc,
            far_remote, near_remote, parent_remote, basis, transfer,
        )

    kinds = "ssss" + "v" * (REACH + 8)
    own, up = call(
        lift_kernel, "vvv", [own_shape, up_shape], [], (values.T, basis, transfer),
        2 * leaves * block,
    )
    first, own, up = call(
        middle_kernel, kinds, [out_shape, own_shape, up_shape], acc_scratch, exchange(own, up),
        150 * block,
    )
    second = call(
        last_kernel, kinds, out_shape, acc_scratch, exchange(own, up), 150 * block
    )
    return first.T, second.T


def solution(mesh):
    return jax.shard_map(
        on_device,
        mesh=mesh,
        in_specs=(
            P(("groups", "clu"), None),
            P(("groups", "clu"), None, None),
            P(("groups", "clu"), None, None),
            P(("groups", "clu"), None),
            P(("groups", "clu"), None, None, None),
            P(("groups", "clu"), None),
            P(("groups", "clu"), None, None, None),
            P(("groups", "clu"), None, None),
            P(("groups", "clu"), None, None, None),
            P(("groups", "clu"), None, None),
            P(("groups", "clu"), None, None, None),
            P(("groups", "clu"), None, None),
            P(("groups", "clu"), None, None, None),
        ),
        out_specs=(P(("groups", "clu"), None), P(("groups", "clu"), None)),
        check_vma=False,
    )
```

```python
import jax
import jax.numpy as jnp
from jax import lax
from jax.experimental import pallas as pl
from jax.experimental.pallas import tpu as pltpu
from jax.sharding import PartitionSpec as P


HOPS = 6
CAP0 = 6
CAPN = 2
FAN = 8
REACH = (HOPS + 1) // 2
OFFSETS = 2 * HOPS
FAR_TILES = CAP0 // 2
PAIR_TILES = (CAP0 + CAPN) // 2
F32 = jnp.float32
BF16 = jnp.bfloat16
VMEM = pl.BlockSpec(memory_space=pltpu.VMEM)
SMEM = pl.BlockSpec(memory_space=pltpu.SMEM)
PARAMS = pltpu.CompilerParams(vmem_limit_bytes=60 * 1024 * 1024)


def nn(a, b):
    return jnp.dot(a, b, preferred_element_type=F32)


def nt(a, b):
    return lax.dot_general(a, b, (((1,), (1,)), ((), ())), preferred_element_type=F32)


def beside(a, b):
    return jnp.concatenate([a, b], axis=1)


def outward(devices, by):
    chips = devices // 2
    up = [(2 * c, 2 * (c + by)) for c in range(chips) if c + by < chips]
    return up + [(2 * c + 1, 2 * (c - by) + 1) for c in range(chips) if c - by >= 0]


def mates(devices):
    return [(i, i ^ 1) for i in range(devices)]


def offset_index(off):
    where = off + HOPS - jnp.where(off > 0, 1, 0)
    return jnp.clip(where, 0, OFFSETS - 1)


def lift_tiles(tiles, basis, transfer, own, up):
    count = len(tiles)
    sums = []
    for i, tile in enumerate(tiles):
        width = basis.shape[1]
        c0 = nn(tile[:, :width], basis[2 * i])
        c1 = nn(tile[:, width:], basis[2 * i + 1])
        coarse = beside(c0, c1).astype(BF16)
        own[i] = coarse
        own[count + i] = tile
        part = nn(coarse[:, :width], transfer[2 * i]) + nn(coarse[:, width:], transfer[2 * i + 1])
        if i % (FAN // 2) == 0:
            sums.append(part)
        else:
            sums[-1] = sums[-1] + part
    parents = beside(*sums).astype(BF16)
    for c in range(up.shape[0]):
        up[c] = parents


def lift_kernel(values, basis, transfer, own, up):
    tiles = [values[:, 128 * i : 128 * (i + 1)] for i in range(values.shape[1] // 128)]
    lift_tiles(tiles, basis, transfer, own, up)


def turn_tables(sources, table):
    row = 0
    for ref in sources:
        for i in range(ref.shape[0]):
            tile = ref[i]
            table[0, row] = tile
            table[1, row] = beside(tile[:, 64:], tile[:, :64])
            row += 1


def ask_kernel(far_plan, near_plan, out):
    far, near = far_plan[0, 0:1, :], near_plan[0, 0:1, :]
    blank = jnp.zeros((1, 128 - far.shape[1] - near.shape[1]), jnp.int32)
    row = jnp.concatenate([far, near, blank], axis=1)
    for i in range(out.shape[0]):
        out[i] = row


def at_left(table, base, leaf):
    return table[leaf % 2, base + leaf // 2]


def at_right(table, base, leaf):
    return table[1 - leaf % 2, base + leaf // 2]


def pair_of(table, base, first, second, left):
    return jnp.where(left, at_left(table, base, first), at_right(table, base, second))


def left_mask():
    return lax.broadcasted_iota(jnp.int32, (64, 128), 1) < 64


def pack_kernel(place_ref, asks, own, mate, *refs):
    outs, table = refs[:REACH], refs[REACH]
    core, chip = place_ref[0], place_ref[1]
    chips = asks.shape[0] // 2
    turn_tables((own, mate), table)
    left = left_mask()
    half = own.shape[0]
    for step in range(REACH):
        out = outs[step]
        toward = jnp.where(core == 0, -2 * (step + 1), 2 * (step + 1))
        asker = jnp.clip(chip - toward // 2, 0, chips - 1)
        for other_target in range(2):
            target = jnp.where(core == other_target, 0, 1)
            for other_source in range(2):
                source = jnp.where(core == other_source, 0, 1)
                order = offset_index(toward + source - target)
                for i in range(PAIR_TILES):
                    if i < FAR_TILES:
                        at = order * CAP0 + 2 * i
                        base = other_source * half
                    else:
                        at = OFFSETS * CAP0 + order * CAPN + 2 * (i - FAR_TILES)
                        base = other_source * half + half // 2
                    first = jnp.maximum(asks[2 * asker + target, 0, at], 0)
                    second = jnp.maximum(asks[2 * asker + target, 0, at + 1], 0)
                    out[(other_target * 2 + other_source) * PAIR_TILES + i] = pair_of(
                        table, base, first, second, left
                    )


def local_kernel(
    place_ref, far_list, near_list, far_plan, near_plan, own, mate, far_blocks, near_blocks,
    far_remote, near_remote, far_out, near_out, table
):
    core = place_ref[0]
    turn_tables((own, mate), table)
    left = left_mask()
    half = own.shape[0]
    leaves = far_blocks.shape[0]

    def one_leaf(leaf, carry):
        for listed, blocks, out, kind in (
            (far_list, far_blocks, far_out, 0),
            (near_list, near_blocks, near_out, 1),
        ):
            base = kind * (half // 2)
            total = jnp.zeros((64, 64), F32)
            for k in range(0, blocks.shape[1], 2):
                x = pair_of(table, base, listed[k, leaf], listed[k + 1, leaf], left)
                total = total + nt(x, beside(blocks[leaf, k], blocks[leaf, k + 1]))
            out[leaf] = total
        return carry

    lax.fori_loop(0, leaves, one_leaf, 0)
    order = jnp.where(core == 0, HOPS, HOPS - 1)
    for plan, blocks, out, kind, cap in (
        (far_plan, far_remote, far_out, 0, CAP0),
        (near_plan, near_remote, near_out, 1, CAPN),
    ):
        base = half + kind * (half // 2)
        out[leaves] = jnp.zeros((64, 64), F32)
        for c in range(cap):
            slot = order * cap + c
            target = plan[0, 1, slot]
            where = jnp.where(target < 0, leaves, target)
            x = at_left(table, base, jnp.maximum(plan[0, 0, slot], 0))[:, :64]
            out[where] = out[where] + nt(x, blocks[slot])


def combine(
    place_ref, far_plan, near_plan, parent_plan, arrived, parents, swapped, far_in, near_in,
    far_remote, near_remote, parent_remote, basis, transfer, far_acc, near_acc
):
    core = place_ref[0]
    leaves = basis.shape[0]
    per_step = 2 * PAIR_TILES
    far_acc[...] = far_in[...]
    near_acc[...] = near_in[...]
    for step in range(REACH):
        for side in range(2):
            for other in range(2):
                sender = jnp.where(core == side, 0, 1)
                source = jnp.where(sender == other, 0, 1)
                away = jnp.where(sender == 0, -2 * (step + 1), 2 * (step + 1))
                off = away + source - core
                inside = jnp.logical_and(off >= -HOPS, off <= HOPS)
                order = offset_index(off)
                for i in range(PAIR_TILES):
                    row = other * PAIR_TILES + i
                    tile = swapped[step * per_step + row] if side else arrived[step][row]
                    if i < FAR_TILES:
                        plan, blocks, acc = far_plan, far_remote, far_acc
                        slot = order * CAP0 + 2 * i
                    else:
                        plan, blocks, acc = near_plan, near_remote, near_acc
                        slot = order * CAPN + 2 * (i - FAR_TILES)
                    for c in range(2):
                        target = plan[0, 1, slot + c]
                        live = jnp.logical_and(inside, target >= 0)
                        where = jnp.where(live, target, leaves)
                        x = tile[:, 64 * c : 64 * (c + 1)]
                        acc[where] = acc[where] + nt(x, blocks[slot + c])

    chips = parents.shape[0]
    left = left_mask()

    def one_chip(chip, total):
        for side in range(2):
            tile = swapped[REACH * per_step + chip] if side else parents[chip]
            member = jnp.where(core == side, 0, 1)
            turned = beside(tile[:, 64:], tile[:, :64])
            slot = (2 * chip + member) * 2
            s0, s1 = parent_plan[0, 0, slot], parent_plan[0, 0, slot + 1]
            t0, t1 = parent_plan[0, 1, slot], parent_plan[0, 1, slot + 1]
            x0 = jnp.where(s0 > 0, turned, tile)
            x1 = jnp.where(s1 == 0, turned, tile)
            zero = jnp.zeros_like(tile)
            rows = []
            for p in range(2):
                x = jnp.where(left, jnp.where(t0 == p, x0, zero), jnp.where(t1 == p, x1, zero))
                rows.append(x)
            weights = beside(parent_remote[slot], parent_remote[slot + 1])
            total = total + nt(jnp.concatenate(rows, axis=0), weights)
        return total

    total = jnp.zeros((128, 64), F32)
    if chips <= 8:
        for chip in range(chips):
            total = one_chip(chip, total)
    else:
        total = lax.fori_loop(0, chips, one_chip, total)
    parent_sum = total.astype(BF16)

    tiles = []
    for i in range(leaves // 2):
        halves = []
        for leaf in (2 * i, 2 * i + 1):
            p = leaf // FAN
            down = nt(parent_sum[64 * p : 64 * (p + 1)], transfer[leaf])
            summed = (far_acc[leaf] + down).astype(BF16)
            halves.append(nt(summed, basis[leaf]) + near_acc[leaf])
        tiles.append(beside(*halves).astype(BF16))
    return tiles


def split_refs(refs):
    place_ref, far_plan, near_plan, parent_plan = refs[:4]
    arrived = refs[4 : 4 + REACH]
    return (place_ref, far_plan, near_plan, parent_plan, arrived) + tuple(refs[4 + REACH :])


def middle_kernel(*refs):
    out, own, up, far_acc, near_acc = refs[-5:]
    args = split_refs(refs[:-5])
    basis, transfer = refs[-7], refs[-6]
    tiles = combine(*args, far_acc, near_acc)
    for i, tile in enumerate(tiles):
        out[:, 128 * i : 128 * (i + 1)] = tile
    lift_tiles(tiles, basis, transfer, own, up)


def last_kernel(*refs):
    out, far_acc, near_acc = refs[-3:]
    tiles = combine(*split_refs(refs[:-3]), far_acc, near_acc)
    for i, tile in enumerate(tiles):
        out[:, 128 * i : 128 * (i + 1)] = tile


def call(kernel, kinds, outs, scratch, args, flops):
    size = sum(a.size * a.dtype.itemsize for a in args)
    return pl.pallas_call(
        kernel,
        out_shape=outs,
        in_specs=[SMEM if k == "s" else VMEM for k in kinds],
        out_specs=jax.tree.map(lambda _: VMEM, outs),
        scratch_shapes=scratch,
        compiler_params=PARAMS,
        cost_estimate=pl.CostEstimate(flops=int(flops), bytes_accessed=size, transcendentals=0),
    )(*args)


def on_device(
    values,
    basis,
    transfer,
    near_list,
    near_blocks,
    far_list,
    far_blocks,
    near_plan,
    near_remote,
    far_plan,
    far_remote,
    parent_plan,
    parent_remote,
):
    devices = lax.axis_size("clu")
    chips = devices // 2
    leaves = basis.shape[0]
    at = lax.axis_index("clu").astype(jnp.int32)
    place = jnp.stack([at & 1, at >> 1])
    near_remote, far_remote, parent_remote = near_remote[0], far_remote[0], parent_remote[0]
    far_list, near_list = far_list.T, near_list.T
    same_core = [[2 * c + k for c in range(chips)] for k in range(2)]

    shape = jax.ShapeDtypeStruct
    own_shape = shape((leaves, 64, 128), BF16)
    up_shape = shape((chips, 64, 128), BF16)
    out_shape = shape((64, values.shape[0]), BF16)
    acc_shape = shape((leaves + 1, 64, 64), F32)
    acc_scratch = [pltpu.VMEM((leaves + 1, 64, 64), F32)] * 2
    table_scratch = [pltpu.VMEM((2, 2 * leaves, 64, 128), BF16)]
    message = shape((4 * PAIR_TILES, 64, 128), BF16)
    block = 2 * 64**3

    asks = call(
        ask_kernel, "vv", shape((devices, 1, 128), jnp.int32), [], (far_plan, near_plan), 1000
    )
    asks = lax.all_to_all(asks, "clu", 0, 0, tiled=True)

    def exchange(own, up):
        parents = lax.all_to_all(up, "clu", 0, 0, tiled=True, axis_index_groups=same_core)
        mate = lax.ppermute(own, "clu", mates(devices))
        packed = call(
            pack_kernel, "ssvv", [message] * REACH, table_scratch, (place, asks, own, mate), 2e9
        )
        arrived = [
            lax.ppermute(m, "clu", outward(devices, d + 1)) for d, m in enumerate(packed)
        ]
        far_acc, near_acc = call(
            local_kernel, "sssss" + "v" * 6, [acc_shape] * 2, table_scratch,
            (place, far_list, near_list, far_plan, near_plan, own, mate, far_blocks, near_blocks,
             far_remote, near_remote),
            7e9,
        )
        arrived, parents, far_acc, near_acc = lax.optimization_barrier(
            (arrived, parents, far_acc, near_acc)
        )
        swapped = jnp.concatenate([m[2 * PAIR_TILES :] for m in arrived] + [parents])
        swapped = lax.ppermute(swapped, "clu", mates(devices))
        return (
            place, far_plan, near_plan, parent_plan, *arrived, parents, swapped, far_acc,
            near_acc, far_remote, near_remote, parent_remote, basis, transfer,
        )

    kinds = "ssss" + "v" * (REACH + 9)
    own, up = call(
        lift_kernel, "vvv", [own_shape, up_shape], [], (values.T, basis, transfer),
        1e9,
    )
    first, own, up = call(
        middle_kernel, kinds, [out_shape, own_shape, up_shape], acc_scratch, exchange(own, up),
        4e9,
    )
    second = call(
        last_kernel, kinds, out_shape, acc_scratch, exchange(own, up), 4e9
    )
    return first.T, second.T


def solution(mesh):
    return jax.shard_map(
        on_device,
        mesh=mesh,
        in_specs=(
            P(("groups", "clu"), None),
            P(("groups", "clu"), None, None),
            P(("groups", "clu"), None, None),
            P(("groups", "clu"), None),
            P(("groups", "clu"), None, None, None),
            P(("groups", "clu"), None),
            P(("groups", "clu"), None, None, None),
            P(("groups", "clu"), None, None),
            P(("groups", "clu"), None, None, None),
            P(("groups", "clu"), None, None),
            P(("groups", "clu"), None, None, None),
            P(("groups", "clu"), None, None),
            P(("groups", "clu"), None, None, None),
        ),
        out_specs=(P(("groups", "clu"), None), P(("groups", "clu"), None)),
        check_vma=False,
    )
```

```python
import jax
import jax.numpy as jnp
from jax import lax
from jax.experimental import pallas as pl
from jax.experimental.pallas import tpu as pltpu
from jax.sharding import PartitionSpec as P


HOPS = 6
CAP0 = 6
CAPN = 2
FAN = 8
REACH = (HOPS + 1) // 2
OFFSETS = 2 * HOPS
FAR_TILES = CAP0 // 2
PAIR_TILES = (CAP0 + CAPN) // 2
F32 = jnp.float32
BF16 = jnp.bfloat16
VMEM = pl.BlockSpec(memory_space=pltpu.VMEM)
SMEM = pl.BlockSpec(memory_space=pltpu.SMEM)
ANY = pl.BlockSpec(memory_space=pl.ANY)
HBM = pl.BlockSpec(memory_space=pltpu.HBM)
MIB = 1024 * 1024
SPECS = {"s": SMEM, "v": VMEM, "a": ANY, "h": HBM}
PAIRS = [[(0, 0), (0, 1), (1, 0), (1, 1)]] * (REACH - 1) + [[(0, 0), (0, 1), (1, 1)]]
MINE = 2 * PAIR_TILES
MATES = [PAIR_TILES * (len(p) - 2) for p in PAIRS]


def nn(a, b):
    return jnp.dot(a, b, preferred_element_type=F32)


def nt(a, b):
    return lax.dot_general(a, b, (((1,), (1,)), ((), ())), preferred_element_type=F32)


def beside(a, b):
    return jnp.concatenate([a, b], axis=1)


def outward(devices, by):
    chips = devices // 2
    up = [(2 * c, 2 * (c + by)) for c in range(chips) if c + by < chips]
    return up + [(2 * c + 1, 2 * (c - by) + 1) for c in range(chips) if c - by >= 0]


def mates(devices):
    return [(i, i ^ 1) for i in range(devices)]


def offset_index(off):
    where = off + HOPS - jnp.where(off > 0, 1, 0)
    return jnp.clip(where, 0, OFFSETS - 1)


def lift_tiles(tiles, basis, transfer, own, up):
    count = len(tiles)
    sums = []
    for i, tile in enumerate(tiles):
        width = basis.shape[1]
        c0 = nn(tile[:, :width], basis[2 * i])
        c1 = nn(tile[:, width:], basis[2 * i + 1])
        coarse = beside(c0, c1).astype(BF16)
        own[i] = coarse
        own[count + i] = tile
        part = nn(coarse[:, :width], transfer[2 * i]) + nn(coarse[:, width:], transfer[2 * i + 1])
        if i % (FAN // 2) == 0:
            sums.append(part)
        else:
            sums[-1] = sums[-1] + part
    parents = beside(*sums).astype(BF16)
    for c in range(up.shape[0]):
        up[c, 0:64, :] = parents


def cut(values):
    return [values[:, 128 * i : 128 * (i + 1)] for i in range(values.shape[1] // 128)]


def lift_kernel(*refs):
    inputs, (own, up), loaded, sems = refs[:5], refs[5:7], refs[7:12], refs[12]
    copies = fetch(list(zip(inputs, loaded)), sems)
    for copy in copies:
        copy.wait()
    values, basis, transfer, far_plan, near_plan = loaded
    lift_tiles(cut(values), basis, transfer, own, up)
    far, near = far_plan[0, 0:1, :], near_plan[0, 0:1, :]
    blank = jnp.zeros((1, 128 - far.shape[1] - near.shape[1]), jnp.int32)
    row = jnp.concatenate([far, near, blank], axis=1).astype(F32)
    rows = jnp.broadcast_to(row, (up.shape[1] - 64, 128)).astype(BF16)
    for c in range(up.shape[0]):
        up[c, 64:, :] = rows


def turn_tables(sources, table):
    row = 0
    for ref in sources:
        for i in range(ref.shape[0]):
            tile = ref[i]
            table[0, row] = tile
            table[1, row] = beside(tile[:, 64:], tile[:, :64])
            row += 1


def at_left(table, base, leaf):
    return table[leaf % 2, base + leaf // 2]


def at_right(table, base, leaf):
    return table[1 - leaf % 2, base + leaf // 2]


def pair_of(table, base, first, second, left):
    return jnp.where(left, at_left(table, base, first), at_right(table, base, second))


def left_mask():
    return lax.broadcasted_iota(jnp.int32, (64, 128), 1) < 64


def pack_kernel(place_ref, asks, mate_asks, own, mate, *refs):
    outs, table = refs[:REACH], refs[REACH]
    core, chip = place_ref[0], place_ref[1]
    chips = asks.shape[0]
    turn_tables((own, mate), table)
    left = left_mask()
    half = own.shape[0]
    for step in range(REACH):
        toward = jnp.where(core == 0, -2 * (step + 1), 2 * (step + 1))
        asker = jnp.clip(chip - toward // 2, 0, chips - 1)
        for place, (other_target, other_source) in enumerate(PAIRS[step]):
            target = jnp.where(core == other_target, 0, 1)
            source = jnp.where(core == other_source, 0, 1)
            order = offset_index(toward + source - target)
            asked = mate_asks if other_target else asks
            for i in range(PAIR_TILES):
                if i < FAR_TILES:
                    at = order * CAP0 + 2 * i
                    base = other_source * half
                else:
                    at = OFFSETS * CAP0 + order * CAPN + 2 * (i - FAR_TILES)
                    base = other_source * half + half // 2
                first = jnp.maximum(asked[asker, at], 0)
                second = jnp.maximum(asked[asker, at + 1], 0)
                outs[step][place * PAIR_TILES + i] = pair_of(table, base, first, second, left)


def fetch(pairs, sems):
    copies = []
    for i, (source, target) in enumerate(pairs):
        copy = pltpu.make_async_copy(source, target, sems.at[i])
        copy.start()
        copies.append(copy)
    return copies


CHUNKS = 4


def local_body(
    place_ref, far_list, near_list, far_plan, near_plan, own_in, mate_in, far_in, near_in, out,
    table, own, mate, far_blocks, near_blocks, sems, far_remote, near_remote, further, lean=False
):
    core = place_ref[0]
    leaves = far_blocks.shape[0]
    step = leaves // CHUNKS
    pairs = [(own_in, own)]
    for c in range(CHUNKS):
        rows = pl.ds(c * step, step)
        pairs += [(far_in.at[rows], far_blocks.at[rows]), (near_in.at[rows], near_blocks.at[rows])]
    order = jnp.where(core == 0, HOPS, HOPS - 1)
    if lean:
        (far_from, far_to), (near_from, near_to) = further
        further = [
            (far_from.at[pl.ds(order * CAP0, CAP0)], far_to),
            (near_from.at[pl.ds(order * CAPN, CAPN)], near_to),
        ]
    copies = fetch(pairs + [(mate_in, mate)] + further, sems)
    copies[0].wait()
    turn_tables((own,), table)
    left = left_mask()
    half = own.shape[0]
    for leaf in range(leaves):
        if leaf % step == 0:
            c = leaf // step
            copies[1 + 2 * c].wait()
            copies[2 + 2 * c].wait()
        sums = []
        for listed, blocks, base in (
            (far_list, far_blocks, 0),
            (near_list, near_blocks, half // 2),
        ):
            xs, ws = [], []
            for k in range(0, blocks.shape[1], 2):
                xs.append(pair_of(table, base, listed[k, leaf], listed[k + 1, leaf], left))
                ws.append(beside(blocks[leaf, k], blocks[leaf, k + 1]))
            sums.append(nt(jnp.concatenate(xs, axis=1), jnp.concatenate(ws, axis=1)))
        out[leaf] = beside(*sums)
    for copy in copies[1 + 2 * CHUNKS :]:
        copy.wait()
    out[leaves] = jnp.zeros((64, 128), F32)
    for plan, blocks, base, cap in (
        (far_plan, far_remote, 0, CAP0),
        (near_plan, near_remote, half // 2, CAPN),
    ):
        for c in range(cap):
            slot = order * cap + c
            target = plan[0, 1, slot]
            where = jnp.where(target < 0, leaves, target)
            leaf = jnp.maximum(plan[0, 0, slot], 0)
            tile = mate[base + leaf // 2]
            x = jnp.where(leaf % 2 == 0, tile[:, :64], tile[:, 64:])
            w = blocks[c if lean else slot]
            z = jnp.zeros_like(w)
            w = jnp.concatenate([z, w] if base else [w, z], axis=0)
            out[where] = out[where] + nt(x, w)


def local_kernel(*refs):
    ins, statics, out, held, scratch = refs[:9], refs[9:14], refs[14], refs[15:20], refs[20:]
    local_body(*ins, out, *scratch, held[0], held[1], list(zip(statics, held)))


def lean_local_kernel(*refs):
    ins, remote, out, scratch, held = refs[:9], refs[9:11], refs[11], refs[12:18], refs[18:]
    local_body(*ins, out, *scratch, *held, list(zip(remote, held)), lean=True)


def combine(
    place_ref, far_plan, near_plan, parent_plan, arrived_in, parents_in, swapped_in, sums,
    far_remote, near_remote, parent_remote, basis, transfer,
    arrived, parents, swapped, far_acc, near_acc, sems, later=()
):
    core = place_ref[0]
    leaves = basis.shape[0]
    copies = fetch(
        [(swapped_in, swapped), (parents_in.at[:, pl.ds(0, 64)], parents)]
        + [(a.at[pl.ds(0, MINE)], arrived.at[i]) for i, a in enumerate(arrived_in)]
        + list(later),
        sems,
    )
    far_acc[...] = jnp.zeros(far_acc.shape, F32)
    near_acc[...] = jnp.zeros(near_acc.shape, F32)
    first = 2 + REACH + len(later) // 3
    for copy in copies[:first]:
        copy.wait()
    row = 0
    for step in range(REACH):
        for side in range(2):
            for other_target, other in PAIRS[step]:
                if other_target != side:
                    continue
                sender = jnp.where(core == side, 0, 1)
                source = jnp.where(sender == other, 0, 1)
                away = jnp.where(sender == 0, -2 * (step + 1), 2 * (step + 1))
                order = offset_index(away + source - core)
                for i in range(PAIR_TILES):
                    if side:
                        tile = swapped[row]
                        row += 1
                    else:
                        tile = arrived[step, other * PAIR_TILES + i]
                    if i < FAR_TILES:
                        plan, blocks, acc = far_plan, far_remote, far_acc
                        slot = order * CAP0 + 2 * i
                    else:
                        plan, blocks, acc = near_plan, near_remote, near_acc
                        slot = order * CAPN + 2 * (i - FAR_TILES)
                    b0, b1 = blocks[slot], blocks[slot + 1]
                    zero = jnp.zeros_like(b0)
                    y = nt(tile, jnp.concatenate([beside(b0, zero), beside(zero, b1)], axis=0))
                    t0, t1 = plan[0, 1, slot], plan[0, 1, slot + 1]
                    t0, t1 = jnp.where(t0 < 0, leaves, t0), jnp.where(t1 < 0, leaves, t1)
                    acc[t0, :, 0:64] = acc[t0, :, 0:64] + y[:, 0:64]
                    acc[t1, :, 64:128] = acc[t1, :, 64:128] + y[:, 64:128]

    chips = parents.shape[0]
    left = left_mask()
    mates_parents = row
    for copy in copies[first:]:
        copy.wait()

    def one_chip(chip, total):
        xs, ws = [], []
        for side in range(2):
            tile = swapped[mates_parents + chip] if side else parents[chip]
            member = jnp.where(core == side, 0, 1)
            turned = beside(tile[:, 64:], tile[:, :64])
            slot = (2 * chip + member) * 2
            s0, s1 = parent_plan[0, 0, slot], parent_plan[0, 0, slot + 1]
            t0, t1 = parent_plan[0, 1, slot], parent_plan[0, 1, slot + 1]
            x0 = jnp.where(s0 > 0, turned, tile)
            x1 = jnp.where(s1 == 0, turned, tile)
            zero = jnp.zeros_like(tile)
            rows = []
            for p in range(2):
                x = jnp.where(left, jnp.where(t0 == p, x0, zero), jnp.where(t1 == p, x1, zero))
                rows.append(x)
            xs.append(jnp.concatenate(rows, axis=0))
            ws.append(beside(parent_remote[slot], parent_remote[slot + 1]))
        return total + nt(beside(*xs), beside(*ws))

    total = jnp.zeros((128, 64), F32)
    if chips <= 8:
        for chip in range(chips):
            total = one_chip(chip, total)
    else:
        total = lax.fori_loop(0, chips, one_chip, total)
    parent_sum = total.astype(BF16)

    tiles = []
    for i in range(leaves // 2):
        halves = []
        for leaf in (2 * i, 2 * i + 1):
            p = leaf // FAN
            down = nt(parent_sum[64 * p : 64 * (p + 1)], transfer[leaf])
            here, far, near = sums[leaf], far_acc[leaf], near_acc[leaf]
            summed = (here[:, :64] + far[:, :64] + far[:, 64:] + down).astype(BF16)
            rest = here[:, 64:] + near[:, :64] + near[:, 64:]
            halves.append(nt(summed, basis[leaf]) + rest)
        tiles.append(beside(*halves).astype(BF16))
    return tiles


def split_refs(refs):
    return tuple(refs[:4]) + (refs[4 : 4 + REACH],) + tuple(refs[4 + REACH :])


def middle_kernel(*refs):
    inputs, (out, own, up), scratch = refs[:-9], refs[-9:-6], refs[-6:]
    basis, transfer = inputs[-2:]
    tiles = combine(*split_refs(inputs), *scratch)
    for i, tile in enumerate(tiles):
        out[:, 128 * i : 128 * (i + 1)] = tile
    lift_tiles(tiles, basis, transfer, own, up)


def last_kernel(*refs):
    sent = 4 + REACH + 2
    inputs, statics, rest = refs[:sent], refs[sent : sent + 6], refs[sent + 6 :]
    out, scratch, held = rest[0], rest[1:7], rest[7:]
    later = [(statics[i], held[i]) for i in (1, 2, 3, 0, 4, 5)]
    tiles = combine(*split_refs(inputs + held), *scratch, later)
    for i, tile in enumerate(tiles):
        out[:, 128 * i : 128 * (i + 1)] = tile


def call(kernel, kinds, outs, scratch, args, flops, limit=24):
    size = sum(a.size * a.dtype.itemsize for a in args)
    return pl.pallas_call(
        kernel,
        out_shape=outs,
        in_specs=[SPECS[k] for k in kinds],
        out_specs=jax.tree.map(lambda _: VMEM, outs),
        scratch_shapes=scratch,
        compiler_params=pltpu.CompilerParams(vmem_limit_bytes=limit * MIB),
        cost_estimate=pl.CostEstimate(flops=int(flops), bytes_accessed=size, transcendentals=0),
    )(*args)


def on_device(
    values,
    basis,
    transfer,
    near_list,
    near_blocks,
    far_list,
    far_blocks,
    near_plan,
    near_remote,
    far_plan,
    far_remote,
    parent_plan,
    parent_remote,
):
    devices = lax.axis_size("clu")
    chips = devices // 2
    leaves = basis.shape[0]
    at = lax.axis_index("clu").astype(jnp.int32)
    place = jnp.stack([at & 1, at >> 1])
    near_remote, far_remote, parent_remote = near_remote[0], far_remote[0], parent_remote[0]
    far_list, near_list = far_list.T, near_list.T
    same_core = [[2 * c + k for c in range(chips)] for k in range(2)]

    shape = jax.ShapeDtypeStruct
    dma = pltpu.SemaphoreType.DMA
    own_shape = shape((leaves, 64, 128), BF16)
    out_shape = shape((64, values.shape[0]), BF16)
    sums_shape = shape((leaves + 1, 64, 128), F32)
    statics = (far_remote, near_remote, parent_remote, basis, transfer)
    held_shapes = [pltpu.VMEM(x.shape, x.dtype) for x in statics]
    table_scratch = [pltpu.VMEM((2, 2 * leaves, 64, 128), BF16)]
    local_scratch = [
        pltpu.VMEM((2, leaves, 64, 128), BF16),
        pltpu.VMEM(own_shape.shape, BF16),
        pltpu.VMEM(own_shape.shape, BF16),
        pltpu.VMEM(far_blocks.shape, BF16),
        pltpu.VMEM(near_blocks.shape, BF16),
    ]
    combine_scratch = [
        pltpu.VMEM((REACH, MINE, 64, 128), BF16),
        pltpu.VMEM((chips, 64, 128), BF16),
        pltpu.VMEM((sum(MATES) + chips, 64, 128), BF16),
        pltpu.VMEM((leaves + 1, 64, 128), F32),
        pltpu.VMEM((leaves + 1, 64, 128), F32),
        dma((2 + REACH,)),
    ]
    messages = [shape((PAIR_TILES * len(p), 64, 128), BF16) for p in PAIRS]

    def crosswise(x):
        return lax.ppermute(x, "clu", mates(devices))

    def exchange(own, up, asks, last):
        parents = lax.all_to_all(up, "clu", 0, 0, tiled=True, axis_index_groups=same_core)
        mate = crosswise(own)
        if asks is None:
            asks = parents[:, 64, :].astype(jnp.int32)
            asks = (asks, crosswise(asks))
        packed = call(
            pack_kernel, "sssvv", messages, table_scratch, (place, *asks, own, mate), 2e9
        )
        arrived = [
            lax.ppermute(m, "clu", outward(devices, d + 1)) for d, m in enumerate(packed)
        ]
        local = (place, far_list, near_list, far_plan, near_plan, own, mate, far_blocks,
                 near_blocks)
        if last:
            held = statics
            sums = call(
                lean_local_kernel, "sssssaahhhh", sums_shape,
                local_scratch + [dma((4 + 2 * CHUNKS,))]
                + [pltpu.VMEM((n, 64, 64), BF16) for n in (CAP0, CAPN)],
                (*local, far_remote, near_remote), 6e9, 60,
            )
        else:
            sums, *held = call(
                local_kernel, "sssssaahh" + "h" * len(statics), [sums_shape, *held_shapes],
                local_scratch + [dma((2 + 2 * CHUNKS + len(statics),))], (*local, *statics), 7e9,
            )
        arrived, parents, sums = lax.optimization_barrier((arrived, parents, sums))
        swapped = jnp.concatenate([m[MINE:] for m in arrived] + [parents[:, :64]])
        swapped = crosswise(swapped)
        inputs = (place, far_plan, near_plan, parent_plan, *arrived, parents, swapped, sums, *held)
        return inputs, asks

    kinds = "ssss" + "a" * (REACH + 2) + "v" * 6
    lifted = (values.T, basis, transfer, far_plan, near_plan)
    own, up = call(
        lift_kernel, "hhhhh", [own_shape, shape((chips, 80, 128), BF16)],
        [pltpu.VMEM(x.shape, x.dtype) for x in lifted] + [dma((len(lifted),))], lifted, 1e9,
        60,
    )
    inputs, asks = exchange(own, up, None, False)
    first, own, up = call(
        middle_kernel, kinds, [out_shape, own_shape, shape((chips, 64, 128), BF16)],
        combine_scratch, inputs, 4e9,
    )
    inputs, _ = exchange(own, up, asks, True)
    loaded = inputs[4 + REACH + 2 :]
    second = call(
        last_kernel, "ssss" + "a" * (REACH + 8), out_shape,
        combine_scratch[:-1] + [dma((2 + REACH + len(loaded),))]
        + [pltpu.VMEM(x.shape, x.dtype) for x in loaded],
        inputs, 4e9, 60,
    )
    return first.T, second.T


def solution(mesh):
    return jax.shard_map(
        on_device,
        mesh=mesh,
        in_specs=(
            P(("groups", "clu"), None),
            P(("groups", "clu"), None, None),
            P(("groups", "clu"), None, None),
            P(("groups", "clu"), None),
            P(("groups", "clu"), None, None, None),
            P(("groups", "clu"), None),
            P(("groups", "clu"), None, None, None),
            P(("groups", "clu"), None, None),
            P(("groups", "clu"), None, None, None),
            P(("groups", "clu"), None, None),
            P(("groups", "clu"), None, None, None),
            P(("groups", "clu"), None, None),
            P(("groups", "clu"), None, None, None),
        ),
        out_specs=(P(("groups", "clu"), None), P(("groups", "clu"), None)),
        check_vma=False,
    )
```

```python
import jax
import jax.numpy as jnp
from jax import lax
from jax.experimental.layout import Layout, with_layout_constraint
from jax.experimental import pallas as pl
from jax.experimental.pallas import tpu as pltpu
from jax.sharding import PartitionSpec as P


HOPS = 6
CAP0 = 6
CAPN = 2
FAN = 8
REACH = (HOPS + 1) // 2
OFFSETS = 2 * HOPS
FAR_TILES = CAP0 // 2
PAIR_TILES = (CAP0 + CAPN) // 2
F32 = jnp.float32
BF16 = jnp.bfloat16
VMEM = pl.BlockSpec(memory_space=pltpu.VMEM)
SMEM = pl.BlockSpec(memory_space=pltpu.SMEM)
ANY = pl.BlockSpec(memory_space=pl.ANY)
HBM = pl.BlockSpec(memory_space=pltpu.HBM)
MIB = 1024 * 1024
SPECS = {"s": SMEM, "v": VMEM, "a": ANY, "h": HBM}
PAIRS = [[(0, 0), (0, 1), (1, 0), (1, 1)]] * (REACH - 1) + [[(0, 0), (0, 1), (1, 1)]]
MINE = 2 * PAIR_TILES


def nn(a, b):
    return jnp.dot(a, b, preferred_element_type=F32)


def nt(a, b):
    return lax.dot_general(a, b, (((1,), (1,)), ((), ())), preferred_element_type=F32)


def beside(a, b):
    return jnp.concatenate([a, b], axis=1)


def outward(devices, by):
    chips = devices // 2
    up = [(2 * c, 2 * (c + by)) for c in range(chips) if c + by < chips]
    return up + [(2 * c + 1, 2 * (c - by) + 1) for c in range(chips) if c - by >= 0]


def mates(devices):
    return [(i, i ^ 1) for i in range(devices)]


def offset_index(off):
    where = off + HOPS - jnp.where(off > 0, 1, 0)
    return jnp.clip(where, 0, OFFSETS - 1)


def lift_tiles(tiles, basis, transfer, own, up):
    count = len(tiles)
    sums = []
    for i, tile in enumerate(tiles):
        width = basis.shape[1]
        c0 = nn(tile[:, :width], basis[2 * i])
        c1 = nn(tile[:, width:], basis[2 * i + 1])
        coarse = beside(c0, c1).astype(BF16)
        own[i] = coarse
        own[count + i] = tile
        part = nn(coarse[:, :width], transfer[2 * i]) + nn(coarse[:, width:], transfer[2 * i + 1])
        if i % (FAN // 2) == 0:
            sums.append(part)
        else:
            sums[-1] = sums[-1] + part
    parents = beside(*sums).astype(BF16)
    for c in range(up.shape[0]):
        up[c, 0:64, :] = parents


def cut(values):
    return [values[:, 128 * i : 128 * (i + 1)] for i in range(values.shape[1] // 128)]


def lift_kernel(*refs):
    inputs, (own, up), loaded, sems = refs[:5], refs[5:7], refs[7:12], refs[12]
    copies = fetch(list(zip(inputs, loaded)), sems)
    for copy in copies:
        copy.wait()
    values, basis, transfer, far_plan, near_plan = loaded
    lift_tiles(cut(values), basis, transfer, own, up)
    far, near = far_plan[0, 0:1, :], near_plan[0, 0:1, :]
    blank = jnp.zeros((1, 128 - far.shape[1] - near.shape[1]), jnp.int32)
    row = jnp.concatenate([far, near, blank], axis=1).astype(F32)
    rows = jnp.broadcast_to(row, (up.shape[1] - 64, 128)).astype(BF16)
    for c in range(up.shape[0]):
        up[c, 64:, :] = rows


def turn_tables(sources, table):
    row = 0
    for ref in sources:
        for i in range(ref.shape[0]):
            tile = ref[i]
            table[0, row] = tile
            table[1, row] = beside(tile[:, 64:], tile[:, :64])
            row += 1


def at_left(table, base, leaf):
    return table[leaf % 2, base + leaf // 2]


def at_right(table, base, leaf):
    return table[1 - leaf % 2, base + leaf // 2]


def pair_of(table, base, first, second, left):
    return jnp.where(left, at_left(table, base, first), at_right(table, base, second))


def left_mask():
    return lax.broadcasted_iota(jnp.int32, (64, 128), 1) < 64


def pack_kernel(place_ref, asks, mate_asks, own, mate, *refs):
    outs, table = refs[:REACH], refs[REACH]
    core, chip = place_ref[0], place_ref[1]
    chips = asks.shape[0]
    turn_tables((own, mate), table)
    left = left_mask()
    half = own.shape[0]
    for step in range(REACH):
        toward = jnp.where(core == 0, -2 * (step + 1), 2 * (step + 1))
        asker = jnp.clip(chip - toward // 2, 0, chips - 1)
        for place, (other_target, other_source) in enumerate(PAIRS[step]):
            target = jnp.where(core == other_target, 0, 1)
            source = jnp.where(core == other_source, 0, 1)
            order = offset_index(toward + source - target)
            asked = mate_asks if other_target else asks
            for i in range(PAIR_TILES):
                if i < FAR_TILES:
                    at = order * CAP0 + 2 * i
                    base = other_source * half
                else:
                    at = OFFSETS * CAP0 + order * CAPN + 2 * (i - FAR_TILES)
                    base = other_source * half + half // 2
                first = jnp.maximum(asked[asker, at], 0)
                second = jnp.maximum(asked[asker, at + 1], 0)
                outs[step][place * PAIR_TILES + i] = pair_of(table, base, first, second, left)


def fetch(pairs, sems):
    copies = []
    for i, (source, target) in enumerate(pairs):
        copy = pltpu.make_async_copy(source, target, sems.at[i])
        copy.start()
        copies.append(copy)
    return copies


CHUNKS = 4


def local_body(
    place_ref, far_list, near_list, far_plan, near_plan, own_in, mate_in, far_in, near_in, out,
    table, own, mate, far_blocks, near_blocks, sems, far_remote, near_remote, further, lean=False
):
    core = place_ref[0]
    leaves = far_blocks.shape[0]
    step = leaves // CHUNKS
    pairs = [(own_in, own)]
    for c in range(CHUNKS):
        rows = pl.ds(c * step, step)
        pairs += [(far_in.at[rows], far_blocks.at[rows]), (near_in.at[rows], near_blocks.at[rows])]
    order = jnp.where(core == 0, HOPS, HOPS - 1)
    if lean:
        (far_from, far_to), (near_from, near_to) = further
        further = [
            (far_from.at[pl.ds(order * CAP0, CAP0)], far_to),
            (near_from.at[pl.ds(order * CAPN, CAPN)], near_to),
        ]
    copies = fetch(pairs + [(mate_in, mate)] + further, sems)
    copies[0].wait()
    turn_tables((own,), table)
    left = left_mask()
    half = own.shape[0]
    for leaf in range(leaves):
        if leaf % step == 0:
            c = leaf // step
            copies[1 + 2 * c].wait()
            copies[2 + 2 * c].wait()
        sums = []
        for listed, blocks, base in (
            (far_list, far_blocks, 0),
            (near_list, near_blocks, half // 2),
        ):
            xs, ws = [], []
            for k in range(0, blocks.shape[1], 2):
                xs.append(pair_of(table, base, listed[k, leaf], listed[k + 1, leaf], left))
                ws.append(beside(blocks[leaf, k], blocks[leaf, k + 1]))
            sums.append(nt(jnp.concatenate(xs, axis=1), jnp.concatenate(ws, axis=1)))
        out[leaf] = beside(*sums)
    for copy in copies[1 + 2 * CHUNKS :]:
        copy.wait()
    out[leaves] = jnp.zeros((64, 128), F32)
    for plan, blocks, base, cap in (
        (far_plan, far_remote, 0, CAP0),
        (near_plan, near_remote, half // 2, CAPN),
    ):
        for c in range(cap):
            slot = order * cap + c
            target = plan[0, 1, slot]
            where = jnp.where(target < 0, leaves, target)
            leaf = jnp.maximum(plan[0, 0, slot], 0)
            tile = mate[base + leaf // 2]
            x = jnp.where(leaf % 2 == 0, tile[:, :64], tile[:, 64:])
            w = blocks[c if lean else slot]
            z = jnp.zeros_like(w)
            w = jnp.concatenate([z, w] if base else [w, z], axis=0)
            out[where] = out[where] + nt(x, w)


def local_kernel(*refs):
    ins, statics, out, held, scratch = refs[:9], refs[9:14], refs[14], refs[15:20], refs[20:]
    local_body(*ins, out, *scratch, held[0], held[1], list(zip(statics, held)))


def lean_local_kernel(*refs):
    ins, remote, out, scratch, held = refs[:9], refs[9:11], refs[11], refs[12:18], refs[18:]
    local_body(*ins, out, *scratch, *held, list(zip(remote, held)), lean=True)


def combine(
    place_ref, far_plan, near_plan, parent_plan, arrived, parents, swapped, sums,
    far_remote, near_remote, parent_remote, basis, transfer, far_acc, near_acc
):
    core = place_ref[0]
    leaves = basis.shape[0]
    far_acc[...] = jnp.zeros(far_acc.shape, F32)
    near_acc[...] = jnp.zeros(near_acc.shape, F32)
    row = 0
    for step in range(REACH):
        for side in range(2):
            for other_target, other in PAIRS[step]:
                if other_target != side:
                    continue
                sender = jnp.where(core == side, 0, 1)
                source = jnp.where(sender == other, 0, 1)
                away = jnp.where(sender == 0, -2 * (step + 1), 2 * (step + 1))
                order = offset_index(away + source - core)
                for i in range(PAIR_TILES):
                    if side:
                        tile = swapped[row]
                        row += 1
                    else:
                        tile = arrived[step][other * PAIR_TILES + i]
                    if i < FAR_TILES:
                        plan, blocks, acc = far_plan, far_remote, far_acc
                        slot = order * CAP0 + 2 * i
                    else:
                        plan, blocks, acc = near_plan, near_remote, near_acc
                        slot = order * CAPN + 2 * (i - FAR_TILES)
                    b0, b1 = blocks[slot], blocks[slot + 1]
                    zero = jnp.zeros_like(b0)
                    y = nt(tile, jnp.concatenate([beside(b0, zero), beside(zero, b1)], axis=0))
                    t0, t1 = plan[0, 1, slot], plan[0, 1, slot + 1]
                    t0, t1 = jnp.where(t0 < 0, leaves, t0), jnp.where(t1 < 0, leaves, t1)
                    acc[t0, :, 0:64] = acc[t0, :, 0:64] + y[:, 0:64]
                    acc[t1, :, 64:128] = acc[t1, :, 64:128] + y[:, 64:128]

    chips = parents.shape[0]
    left = left_mask()
    mates_parents = row

    def one_chip(chip, total):
        xs, ws = [], []
        for side in range(2):
            tile = swapped[mates_parents + chip] if side else parents[chip, 0:64, :]
            member = jnp.where(core == side, 0, 1)
            turned = beside(tile[:, 64:], tile[:, :64])
            slot = (2 * chip + member) * 2
            s0, s1 = parent_plan[0, 0, slot], parent_plan[0, 0, slot + 1]
            t0, t1 = parent_plan[0, 1, slot], parent_plan[0, 1, slot + 1]
            x0 = jnp.where(s0 > 0, turned, tile)
            x1 = jnp.where(s1 == 0, turned, tile)
            zero = jnp.zeros_like(tile)
            rows = []
            for p in range(2):
                x = jnp.where(left, jnp.where(t0 == p, x0, zero), jnp.where(t1 == p, x1, zero))
                rows.append(x)
            xs.append(jnp.concatenate(rows, axis=0))
            ws.append(beside(parent_remote[slot], parent_remote[slot + 1]))
        return total + nt(beside(*xs), beside(*ws))

    total = jnp.zeros((128, 64), F32)
    if chips <= 8:
        for chip in range(chips):
            total = one_chip(chip, total)
    else:
        total = lax.fori_loop(0, chips, one_chip, total)
    parent_sum = total.astype(BF16)

    tiles = []
    for i in range(leaves // 2):
        halves = []
        for leaf in (2 * i, 2 * i + 1):
            p = leaf // FAN
            down = nt(parent_sum[64 * p : 64 * (p + 1)], transfer[leaf])
            here, far, near = sums[leaf], far_acc[leaf], near_acc[leaf]
            summed = (here[:, :64] + far[:, :64] + far[:, 64:] + down).astype(BF16)
            rest = here[:, 64:] + near[:, :64] + near[:, 64:]
            halves.append(nt(summed, basis[leaf]) + rest)
        tiles.append(beside(*halves).astype(BF16))
    return tiles


def split_refs(refs):
    return tuple(refs[:4]) + (refs[4 : 4 + REACH],) + tuple(refs[4 + REACH :])


def middle_kernel(*refs):
    inputs, (out, own, up), scratch = refs[:-5], refs[-5:-2], refs[-2:]
    basis, transfer = inputs[-2:]
    tiles = combine(*split_refs(inputs), *scratch)
    for i, tile in enumerate(tiles):
        out[:, 128 * i : 128 * (i + 1)] = tile
    lift_tiles(tiles, basis, transfer, own, up)


def last_kernel(*refs):
    inputs, out, scratch = refs[:-3], refs[-3], refs[-2:]
    for i, tile in enumerate(combine(*split_refs(inputs), *scratch)):
        out[:, 128 * i : 128 * (i + 1)] = tile


def call(kernel, kinds, outs, scratch, args, flops, limit=24):
    size = sum(a.size * a.dtype.itemsize for a in args)
    return pl.pallas_call(
        kernel,
        out_shape=outs,
        in_specs=[SPECS[k] for k in kinds],
        out_specs=jax.tree.map(lambda _: VMEM, outs),
        scratch_shapes=scratch,
        compiler_params=pltpu.CompilerParams(vmem_limit_bytes=limit * MIB),
        cost_estimate=pl.CostEstimate(flops=int(flops), bytes_accessed=size, transcendentals=0),
    )(*args)


def on_device(
    values,
    basis,
    transfer,
    near_list,
    near_blocks,
    far_list,
    far_blocks,
    near_plan,
    near_remote,
    far_plan,
    far_remote,
    parent_plan,
    parent_remote,
):
    devices = lax.axis_size("clu")
    chips = devices // 2
    leaves = basis.shape[0]
    at = lax.axis_index("clu").astype(jnp.int32)
    place = jnp.stack([at & 1, at >> 1])
    near_remote, far_remote, parent_remote = near_remote[0], far_remote[0], parent_remote[0]
    far_remote = with_layout_constraint(far_remote, Layout((0, 1, 2)))
    far_list, near_list = far_list.T, near_list.T
    same_core = [[2 * c + k for c in range(chips)] for k in range(2)]

    shape = jax.ShapeDtypeStruct
    dma = pltpu.SemaphoreType.DMA
    own_shape = shape((leaves, 64, 128), BF16)
    out_shape = shape((64, values.shape[0]), BF16)
    sums_shape = shape((leaves + 1, 64, 128), F32)
    statics = (far_remote, near_remote, parent_remote, basis, transfer)
    held_shapes = [pltpu.VMEM(x.shape, x.dtype) for x in statics]
    table_scratch = [pltpu.VMEM((2, 2 * leaves, 64, 128), BF16)]
    local_scratch = [
        pltpu.VMEM((2, leaves, 64, 128), BF16),
        pltpu.VMEM(own_shape.shape, BF16),
        pltpu.VMEM(own_shape.shape, BF16),
        pltpu.VMEM(far_blocks.shape, BF16),
        pltpu.VMEM(near_blocks.shape, BF16),
    ]
    combine_scratch = [pltpu.VMEM((leaves + 1, 64, 128), F32)] * 2
    messages = [shape((PAIR_TILES * len(p), 64, 128), BF16) for p in PAIRS]

    def crosswise(x):
        return lax.ppermute(x, "clu", mates(devices))

    def exchange(own, up, asks, last):
        nonlocal far_remote, statics
        parents = lax.all_to_all(up, "clu", 0, 0, tiled=True, axis_index_groups=same_core)
        mate = crosswise(own)
        if asks is None:
            parents, far_remote = lax.optimization_barrier((parents, far_remote))
            statics = (far_remote, *statics[1:])
            asks = parents[:, 64, :].astype(jnp.int32)
            asks = (asks, crosswise(asks))
        packed = call(
            pack_kernel, "sssvv", messages, table_scratch, (place, *asks, own, mate), 2e9
        )
        arrived = [
            lax.ppermute(m, "clu", outward(devices, d + 1)) for d, m in enumerate(packed)
        ]
        local = (place, far_list, near_list, far_plan, near_plan, own, mate, far_blocks,
                 near_blocks)
        if last:
            held = statics
            sums = call(
                lean_local_kernel, "sssssaahhhh", sums_shape,
                local_scratch + [dma((4 + 2 * CHUNKS,))]
                + [pltpu.VMEM((n, 64, 64), BF16) for n in (CAP0, CAPN)],
                (*local, far_remote, near_remote), 6e9, 60,
            )
        else:
            sums, *held = call(
                local_kernel, "sssssaahh" + "h" * len(statics), [sums_shape, *held_shapes],
                local_scratch + [dma((2 + 2 * CHUNKS + len(statics),))], (*local, *statics), 7e9,
            )
        arrived, parents, sums = lax.optimization_barrier((arrived, parents, sums))
        swapped = jnp.concatenate([m[MINE:] for m in arrived] + [parents[:, :64]])
        swapped = crosswise(swapped)
        inputs = (place, far_plan, near_plan, parent_plan, *arrived, parents, swapped, sums, *held)
        return inputs, asks

    kinds = "ssss" + "v" * (REACH + 8)
    lifted = (values.T, basis, transfer, far_plan, near_plan)
    own, up = call(
        lift_kernel, "hhhhh", [own_shape, shape((chips, 80, 128), BF16)],
        [pltpu.VMEM(x.shape, x.dtype) for x in lifted] + [dma((len(lifted),))], lifted, 1e9,
        60,
    )
    inputs, asks = exchange(own, up, None, False)
    first, own, up = call(
        middle_kernel, kinds, [out_shape, own_shape, shape((chips, 64, 128), BF16)],
        combine_scratch, inputs, 4e9,
    )
    inputs, _ = exchange(own, up, asks, True)
    second = call(last_kernel, kinds, out_shape, combine_scratch, inputs, 4e9, 16)
    return first.T, second.T


def solution(mesh):
    return jax.shard_map(
        on_device,
        mesh=mesh,
        in_specs=(
            P(("groups", "clu"), None),
            P(("groups", "clu"), None, None),
            P(("groups", "clu"), None, None),
            P(("groups", "clu"), None),
            P(("groups", "clu"), None, None, None),
            P(("groups", "clu"), None),
            P(("groups", "clu"), None, None, None),
            P(("groups", "clu"), None, None),
            P(("groups", "clu"), None, None, None),
            P(("groups", "clu"), None, None),
            P(("groups", "clu"), None, None, None),
            P(("groups", "clu"), None, None),
            P(("groups", "clu"), None, None, None),
        ),
        out_specs=(P(("groups", "clu"), None), P(("groups", "clu"), None)),
        check_vma=False,
    )
```

```python
import jax
import jax.numpy as jnp
from jax import lax
from jax.experimental.layout import Layout, with_layout_constraint
from jax.experimental import pallas as pl
from jax.experimental.pallas import tpu as pltpu
from jax.sharding import PartitionSpec as P


HOPS = 6
CAP0 = 6
CAPN = 2
FAN = 8
REACH = (HOPS + 1) // 2
OFFSETS = 2 * HOPS
FAR_TILES = CAP0 // 2
PAIR_TILES = (CAP0 + CAPN) // 2
F32 = jnp.float32
BF16 = jnp.bfloat16
VMEM = pl.BlockSpec(memory_space=pltpu.VMEM)
SMEM = pl.BlockSpec(memory_space=pltpu.SMEM)
ANY = pl.BlockSpec(memory_space=pl.ANY)
HBM = pl.BlockSpec(memory_space=pltpu.HBM)
MIB = 1024 * 1024
SPECS = {"s": SMEM, "v": VMEM, "a": ANY, "h": HBM}
PAIRS = [[(0, 0), (0, 1), (1, 0), (1, 1)]] * (REACH - 1) + [[(0, 0), (0, 1), (1, 1)]]
MINE = 2 * PAIR_TILES


def nn(a, b):
    return jnp.dot(a, b, preferred_element_type=F32)


def nt(a, b):
    return lax.dot_general(a, b, (((1,), (1,)), ((), ())), preferred_element_type=F32)


def beside(a, b):
    return jnp.concatenate([a, b], axis=1)


def outward(devices, by):
    chips = devices // 2
    up = [(2 * c, 2 * (c + by)) for c in range(chips) if c + by < chips]
    return up + [(2 * c + 1, 2 * (c - by) + 1) for c in range(chips) if c - by >= 0]


def mates(devices):
    return [(i, i ^ 1) for i in range(devices)]


def offset_index(off):
    where = off + HOPS - jnp.where(off > 0, 1, 0)
    return jnp.clip(where, 0, OFFSETS - 1)


def lift_tiles(tiles, basis, transfer, own, up):
    count = len(tiles)
    sums = []
    for i, tile in enumerate(tiles):
        width = basis.shape[1]
        c0 = nn(tile[:, :width], basis[2 * i])
        c1 = nn(tile[:, width:], basis[2 * i + 1])
        coarse = beside(c0, c1).astype(BF16)
        own[i] = coarse
        own[count + i] = tile
        part = nn(coarse[:, :width], transfer[2 * i]) + nn(coarse[:, width:], transfer[2 * i + 1])
        if i % (FAN // 2) == 0:
            sums.append(part)
        else:
            sums[-1] = sums[-1] + part
    parents = beside(*sums).astype(BF16)
    for c in range(up.shape[0]):
        up[c, 0:64, :] = parents


def cut(values):
    return [values[:, 128 * i : 128 * (i + 1)] for i in range(values.shape[1] // 128)]


def lift_kernel(*refs):
    inputs, (own, up), loaded, sems = refs[:5], refs[5:7], refs[7:12], refs[12]
    copies = fetch(list(zip(inputs, loaded)), sems)
    for copy in copies:
        copy.wait()
    values, basis, transfer, far_plan, near_plan = loaded
    lift_tiles(cut(values), basis, transfer, own, up)
    far, near = far_plan[0, 0:1, :], near_plan[0, 0:1, :]
    blank = jnp.zeros((1, 128 - far.shape[1] - near.shape[1]), jnp.int32)
    row = jnp.concatenate([far, near, blank], axis=1).astype(F32)
    rows = jnp.broadcast_to(row, (up.shape[1] - 64, 128)).astype(BF16)
    for c in range(up.shape[0]):
        up[c, 64:, :] = rows


def turn_tables(sources, table):
    row = 0
    for ref in sources:
        for i in range(ref.shape[0]):
            tile = ref[i]
            table[0, row] = tile
            table[1, row] = beside(tile[:, 64:], tile[:, :64])
            row += 1


def at_left(table, base, leaf):
    return table[leaf % 2, base + leaf // 2]


def at_right(table, base, leaf):
    return table[1 - leaf % 2, base + leaf // 2]


def pair_of(table, base, first, second, left):
    return jnp.where(left, at_left(table, base, first), at_right(table, base, second))


def left_mask():
    return lax.broadcasted_iota(jnp.int32, (64, 128), 1) < 64


def pack_kernel(place_ref, asks, mate_asks, own, mate, *refs):
    outs, table = refs[:REACH], refs[REACH]
    core, chip = place_ref[0], place_ref[1]
    chips = asks.shape[0]
    turn_tables((own, mate), table)
    left = left_mask()
    half = own.shape[0]
    for step in range(REACH):
        toward = jnp.where(core == 0, -2 * (step + 1), 2 * (step + 1))
        asker = jnp.clip(chip - toward // 2, 0, chips - 1)
        for place, (other_target, other_source) in enumerate(PAIRS[step]):
            target = jnp.where(core == other_target, 0, 1)
            source = jnp.where(core == other_source, 0, 1)
            order = offset_index(toward + source - target)
            asked = mate_asks if other_target else asks
            for i in range(PAIR_TILES):
                if i < FAR_TILES:
                    at = order * CAP0 + 2 * i
                    base = other_source * half
                else:
                    at = OFFSETS * CAP0 + order * CAPN + 2 * (i - FAR_TILES)
                    base = other_source * half + half // 2
                first = jnp.maximum(asked[asker, at], 0)
                second = jnp.maximum(asked[asker, at + 1], 0)
                outs[step][place * PAIR_TILES + i] = pair_of(table, base, first, second, left)


def fetch(pairs, sems):
    copies = []
    for i, (source, target) in enumerate(pairs):
        copy = pltpu.make_async_copy(source, target, sems.at[i])
        copy.start()
        copies.append(copy)
    return copies


CHUNKS = 4


def local_body(
    place_ref, far_list, near_list, far_plan, near_plan, own_in, mate_in, far_in, near_in, out,
    table, own, mate, far_blocks, near_blocks, sems, far_remote, near_remote, further, lean=False
):
    core = place_ref[0]
    leaves = far_blocks.shape[0]
    step = leaves // CHUNKS
    pairs = [(own_in, own)]
    for c in range(CHUNKS):
        rows = pl.ds(c * step, step)
        pairs += [(far_in.at[rows], far_blocks.at[rows]), (near_in.at[rows], near_blocks.at[rows])]
    order = jnp.where(core == 0, HOPS, HOPS - 1)
    if lean:
        (far_from, far_to), (near_from, near_to) = further
        further = [
            (far_from.at[pl.ds(order * CAP0, CAP0)], far_to),
            (near_from.at[pl.ds(order * CAPN, CAPN)], near_to),
        ]
    copies = fetch(pairs + [(mate_in, mate)] + further, sems)
    copies[0].wait()
    turn_tables((own,), table)
    left = left_mask()
    half = own.shape[0]
    for leaf in range(leaves):
        if leaf % step == 0:
            c = leaf // step
            copies[1 + 2 * c].wait()
            copies[2 + 2 * c].wait()
        sums = []
        for listed, blocks, base in (
            (far_list, far_blocks, 0),
            (near_list, near_blocks, half // 2),
        ):
            xs, ws = [], []
            for k in range(0, blocks.shape[1], 2):
                xs.append(pair_of(table, base, listed[k, leaf], listed[k + 1, leaf], left))
                ws.append(beside(blocks[leaf, k], blocks[leaf, k + 1]))
            total = nt(jnp.concatenate(xs, axis=1), jnp.concatenate(ws, axis=1))
            sums.append(beside(total, jnp.zeros_like(total)))
        out[0, leaf], out[1, leaf] = sums
    for copy in copies[1 + 2 * CHUNKS :]:
        copy.wait()
    out[:, leaves] = jnp.zeros((2, 64, 128), F32)
    for kind, plan, blocks, base, cap in (
        (0, far_plan, far_remote, 0, CAP0),
        (1, near_plan, near_remote, half // 2, CAPN),
    ):
        for c in range(cap):
            slot = order * cap + c
            target = plan[0, 1, slot]
            where = jnp.where(target < 0, leaves, target)
            leaf = jnp.maximum(plan[0, 0, slot], 0)
            tile = mate[base + leaf // 2]
            x = jnp.where(leaf % 2 == 0, tile[:, :64], tile[:, 64:])
            w = blocks[c if lean else slot]
            out[kind, where, :, 0:64] = out[kind, where, :, 0:64] + nt(x, w)


def local_kernel(*refs):
    ins, statics, out, held, scratch = refs[:9], refs[9:14], refs[14], refs[15:20], refs[20:]
    local_body(*ins, out, *scratch, held[0], held[1], list(zip(statics, held)))


def lean_local_kernel(*refs):
    ins, remote, out, scratch, held = refs[:9], refs[9:11], refs[11], refs[12:18], refs[18:]
    local_body(*ins, out, *scratch, *held, list(zip(remote, held)), lean=True)


def diagonal(b0, b1):
    zero = jnp.zeros_like(b0)
    return jnp.concatenate([beside(b0, zero), beside(zero, b1)], axis=0)


def add_slots(core, side, tile_at, far_plan, near_plan, far_remote, near_remote, acc):
    leaves = acc.shape[1] - 1
    for step in range(REACH):
        for other_target, other in PAIRS[step]:
            if other_target != side:
                continue
            sender = jnp.where(core == side, 0, 1)
            source = jnp.where(sender == other, 0, 1)
            away = jnp.where(sender == 0, -2 * (step + 1), 2 * (step + 1))
            order = offset_index(away + source - core)
            for i in range(PAIR_TILES):
                if i < FAR_TILES:
                    kind, plan, blocks = 0, far_plan, far_remote
                    slot = order * CAP0 + 2 * i
                else:
                    kind, plan, blocks = 1, near_plan, near_remote
                    slot = order * CAPN + 2 * (i - FAR_TILES)
                y = nt(tile_at(step, other, i), diagonal(blocks[slot], blocks[slot + 1]))
                t0, t1 = plan[0, 1, slot], plan[0, 1, slot + 1]
                t0, t1 = jnp.where(t0 < 0, leaves, t0), jnp.where(t1 < 0, leaves, t1)
                acc[kind, t0, :, 0:64] = acc[kind, t0, :, 0:64] + y[:, 0:64]
                acc[kind, t1, :, 64:128] = acc[kind, t1, :, 64:128] + y[:, 64:128]


def add_parents(core, side, chips, tile_at, parent_plan, parent_remote, total):
    left = left_mask()
    member = jnp.where(core == side, 0, 1)

    def one_chip(chip):
        tile = tile_at(chip)
        turned = beside(tile[:, 64:], tile[:, :64])
        slot = (2 * chip + member) * 2
        s0, s1 = parent_plan[0, 0, slot], parent_plan[0, 0, slot + 1]
        t0, t1 = parent_plan[0, 1, slot], parent_plan[0, 1, slot + 1]
        x0 = jnp.where(s0 > 0, turned, tile)
        x1 = jnp.where(s1 == 0, turned, tile)
        zero = jnp.zeros_like(tile)
        rows = []
        for p in range(2):
            x = jnp.where(left, jnp.where(t0 == p, x0, zero), jnp.where(t1 == p, x1, zero))
            rows.append(x)
        return jnp.concatenate(rows, axis=0), beside(parent_remote[slot], parent_remote[slot + 1])

    def two_chips(index, total):
        (x0, w0), (x1, w1) = one_chip(2 * index), one_chip(2 * index + 1)
        return total + nt(beside(x0, x1), beside(w0, w1))

    if chips % 2:
        total = total + nt(*one_chip(chips - 1))
    if chips <= 8:
        for index in range(chips // 2):
            total = two_chips(index, total)
        return total
    return lax.fori_loop(0, chips // 2, two_chips, total)


def arrived_kernel(*refs):
    place_ref, far_plan, near_plan, parent_plan = refs[:4]
    arrived = refs[4 : 4 + REACH]
    parents, _, far_remote, near_remote, parent_remote, acc, total = refs[4 + REACH :]
    core = place_ref[0]
    add_slots(
        core, 0, lambda step, other, i: arrived[step][other * PAIR_TILES + i],
        far_plan, near_plan, far_remote, near_remote, acc,
    )
    total[...] = add_parents(
        core, 0, parents.shape[0], lambda chip: parents[chip, 0:64, :],
        parent_plan, parent_remote, jnp.zeros((128, 64), F32),
    )


def swapped_body(
    place_ref, far_plan, near_plan, parent_plan, swapped, _, total, far_remote, near_remote,
    parent_remote, basis, transfer, acc
):
    core = place_ref[0]
    leaves = basis.shape[0]
    starts, rows = [], 0
    for pairs in PAIRS:
        starts.append(rows)
        rows += PAIR_TILES * (len(pairs) - 2)

    def tile_at(step, other, i):
        order = [o for t, o in PAIRS[step] if t == 1].index(other)
        return swapped[starts[step] + order * PAIR_TILES + i]

    add_slots(core, 1, tile_at, far_plan, near_plan, far_remote, near_remote, acc)
    parent_sum = add_parents(
        core, 1, swapped.shape[0] - rows, lambda chip: swapped[rows + chip],
        parent_plan, parent_remote, total[...],
    ).astype(BF16)
    left = left_mask()

    def leaf_pair(kind, i):
        a, b = acc[kind, 2 * i], acc[kind, 2 * i + 1]
        crossed = jnp.where(left, b, a)
        return jnp.where(left, a, b) + beside(crossed[:, 64:], crossed[:, :64])

    tiles = []
    for i in range(leaves // 2):
        p = 2 * i // FAN
        both = jnp.concatenate([transfer[2 * i], transfer[2 * i + 1]], axis=0)
        down = nt(parent_sum[64 * p : 64 * (p + 1)], both)
        summed = (leaf_pair(0, i) + down).astype(BF16)
        y = nt(summed, diagonal(basis[2 * i], basis[2 * i + 1])) + leaf_pair(1, i)
        tiles.append(y.astype(BF16))
    return tiles


def middle_kernel(*refs):
    inputs, (acc, out, own, up) = refs[:-4], refs[-4:]
    basis, transfer = inputs[-2:]
    tiles = swapped_body(*inputs, acc)
    for i, tile in enumerate(tiles):
        out[:, 128 * i : 128 * (i + 1)] = tile
    lift_tiles(tiles, basis, transfer, own, up)


def last_kernel(*refs):
    inputs, (acc, out) = refs[:-2], refs[-2:]
    for i, tile in enumerate(swapped_body(*inputs, acc)):
        out[:, 128 * i : 128 * (i + 1)] = tile


def call(kernel, kinds, outs, scratch, args, flops, limit=24, aliases=None):
    size = sum(a.size * a.dtype.itemsize for a in args)
    return pl.pallas_call(
        kernel,
        out_shape=outs,
        in_specs=[SPECS[k] for k in kinds],
        out_specs=jax.tree.map(lambda _: VMEM, outs),
        scratch_shapes=scratch,
        input_output_aliases=aliases or {},
        compiler_params=pltpu.CompilerParams(vmem_limit_bytes=limit * MIB),
        cost_estimate=pl.CostEstimate(flops=int(flops), bytes_accessed=size, transcendentals=0),
    )(*args)


def on_device(
    values,
    basis,
    transfer,
    near_list,
    near_blocks,
    far_list,
    far_blocks,
    near_plan,
    near_remote,
    far_plan,
    far_remote,
    parent_plan,
    parent_remote,
):
    devices = lax.axis_size("clu")
    chips = devices // 2
    leaves = basis.shape[0]
    at = lax.axis_index("clu").astype(jnp.int32)
    place = jnp.stack([at & 1, at >> 1])
    near_remote, far_remote, parent_remote = near_remote[0], far_remote[0], parent_remote[0]
    far_remote = with_layout_constraint(far_remote, Layout((0, 1, 2)))
    far_list, near_list = far_list.T, near_list.T
    same_core = [[2 * c + k for c in range(chips)] for k in range(2)]

    shape = jax.ShapeDtypeStruct
    dma = pltpu.SemaphoreType.DMA
    own_shape = shape((leaves, 64, 128), BF16)
    out_shape = shape((64, values.shape[0]), BF16)
    sums_shape = shape((2, leaves + 1, 64, 128), F32)
    statics = (far_remote, near_remote, parent_remote, basis, transfer)
    held_shapes = [pltpu.VMEM(x.shape, x.dtype) for x in statics]
    table_scratch = [pltpu.VMEM((2, 2 * leaves, 64, 128), BF16)]
    local_scratch = [
        pltpu.VMEM((2, leaves, 64, 128), BF16),
        pltpu.VMEM(own_shape.shape, BF16),
        pltpu.VMEM(own_shape.shape, BF16),
        pltpu.VMEM(far_blocks.shape, BF16),
        pltpu.VMEM(near_blocks.shape, BF16),
    ]
    messages = [shape((PAIR_TILES * len(p), 64, 128), BF16) for p in PAIRS]

    def crosswise(x):
        return lax.ppermute(x, "clu", mates(devices))

    def exchange(own, up, asks, last):
        nonlocal far_remote, statics
        parents = lax.all_to_all(up, "clu", 0, 0, tiled=True, axis_index_groups=same_core)
        mate = crosswise(own)
        if asks is None:
            parents, far_remote = lax.optimization_barrier((parents, far_remote))
            statics = (far_remote, *statics[1:])
            asks = parents[:, 64, :].astype(jnp.int32)
            asks = (asks, crosswise(asks))
        packed = call(
            pack_kernel, "sssvv", messages, table_scratch, (place, *asks, own, mate), 2e9
        )
        arrived = [
            lax.ppermute(m, "clu", outward(devices, d + 1)) for d, m in enumerate(packed)
        ]
        local = (place, far_list, near_list, far_plan, near_plan, own, mate, far_blocks,
                 near_blocks)
        if last:
            held = statics
            sums = call(
                lean_local_kernel, "sssssaahhhh", sums_shape,
                local_scratch + [dma((4 + 2 * CHUNKS,))]
                + [pltpu.VMEM((n, 64, 64), BF16) for n in (CAP0, CAPN)],
                (*local, far_remote, near_remote), 6e9, 12,
            )
        else:
            sums, *held = call(
                local_kernel, "sssssaahh" + "h" * len(statics), [sums_shape, *held_shapes],
                local_scratch + [dma((2 + 2 * CHUNKS + len(statics),))], (*local, *statics), 7e9,
            )
        arrived, parents, sums = lax.optimization_barrier((arrived, parents, sums))
        swapped = jnp.concatenate([m[MINE:] for m in arrived] + [parents[:, :64]])
        swapped = crosswise(swapped)
        plans = (place, far_plan, near_plan, parent_plan)
        sums, total = call(
            arrived_kernel, "ssss" + "v" * (REACH + 5), [sums_shape, shape((128, 64), F32)], [],
            (*plans, *arrived, parents, sums, *held[:3]), 2e9, 16, {4 + REACH + 1: 0},
        )
        return (*plans, swapped, sums, total, *held), asks

    kinds = "ssss" + "v" * 8
    lifted = (values.T, basis, transfer, far_plan, near_plan)
    own, up = call(
        lift_kernel, "hhhhh", [own_shape, shape((chips, 80, 128), BF16)],
        [pltpu.VMEM(x.shape, x.dtype) for x in lifted] + [dma((len(lifted),))], lifted, 1e9,
        60,
    )
    inputs, asks = exchange(own, up, None, False)
    _, first, own, up = call(
        middle_kernel, kinds, [sums_shape, out_shape, own_shape, shape((chips, 64, 128), BF16)],
        [], inputs, 3e9, 16, {5: 0},
    )
    inputs, _ = exchange(own, up, asks, True)
    _, second = call(
        last_kernel, kinds, [sums_shape, out_shape], [], inputs, 2e9, 16, {5: 0}
    )
    return first.T, second.T


def solution(mesh):
    return jax.shard_map(
        on_device,
        mesh=mesh,
        in_specs=(
            P(("groups", "clu"), None),
            P(("groups", "clu"), None, None),
            P(("groups", "clu"), None, None),
            P(("groups", "clu"), None),
            P(("groups", "clu"), None, None, None),
            P(("groups", "clu"), None),
            P(("groups", "clu"), None, None, None),
            P(("groups", "clu"), None, None),
            P(("groups", "clu"), None, None, None),
            P(("groups", "clu"), None, None),
            P(("groups", "clu"), None, None, None),
            P(("groups", "clu"), None, None),
            P(("groups", "clu"), None, None, None),
        ),
        out_specs=(P(("groups", "clu"), None), P(("groups", "clu"), None)),
        check_vma=False,
    )
```

```python
import jax
import jax.numpy as jnp
from jax import lax
from jax.experimental.layout import Layout, with_layout_constraint
from jax.experimental import pallas as pl
from jax.experimental.pallas import tpu as pltpu
from jax.sharding import PartitionSpec as P


HOPS = 6
CAP0 = 6
CAPN = 2
FAN = 8
REACH = (HOPS + 1) // 2
OFFSETS = 2 * HOPS
FAR_TILES = CAP0 // 2
PAIR_TILES = (CAP0 + CAPN) // 2
F32 = jnp.float32
BF16 = jnp.bfloat16
VMEM = pl.BlockSpec(memory_space=pltpu.VMEM)
SMEM = pl.BlockSpec(memory_space=pltpu.SMEM)
ANY = pl.BlockSpec(memory_space=pl.ANY)
HBM = pl.BlockSpec(memory_space=pltpu.HBM)
MIB = 1024 * 1024
SPECS = {"s": SMEM, "v": VMEM, "a": ANY, "h": HBM}
PAIRS = [[(0, 0), (0, 1), (1, 0), (1, 1)]] * (REACH - 1) + [[(0, 0), (0, 1), (1, 1)]]
MINE = 2 * PAIR_TILES


def nn(a, b):
    return jnp.dot(a, b, preferred_element_type=F32)


def nt(a, b):
    return lax.dot_general(a, b, (((1,), (1,)), ((), ())), preferred_element_type=F32)


def beside(a, b):
    return jnp.concatenate([a, b], axis=1)


def outward(devices, by):
    chips = devices // 2
    up = [(2 * c, 2 * (c + by)) for c in range(chips) if c + by < chips]
    return up + [(2 * c + 1, 2 * (c - by) + 1) for c in range(chips) if c - by >= 0]


def mates(devices):
    return [(i, i ^ 1) for i in range(devices)]


def offset_index(off):
    where = off + HOPS - jnp.where(off > 0, 1, 0)
    return jnp.clip(where, 0, OFFSETS - 1)


def lift_tiles(tiles, basis, transfer, own, up):
    count = len(tiles)
    sums = []
    for i, tile in enumerate(tiles):
        width = basis.shape[1]
        c0 = nn(tile[:, :width], basis[2 * i])
        c1 = nn(tile[:, width:], basis[2 * i + 1])
        coarse = beside(c0, c1).astype(BF16)
        own[i] = coarse
        own[count + i] = tile
        part = nn(coarse[:, :width], transfer[2 * i]) + nn(coarse[:, width:], transfer[2 * i + 1])
        if i % (FAN // 2) == 0:
            sums.append(part)
        else:
            sums[-1] = sums[-1] + part
    parents = beside(*sums).astype(BF16)
    for c in range(up.shape[0]):
        up[c, 0:64, :] = parents


def cut(values):
    return [values[:, 128 * i : 128 * (i + 1)] for i in range(values.shape[1] // 128)]


def lift_kernel(*refs):
    inputs, (own, up), loaded, sems = refs[:5], refs[5:7], refs[7:12], refs[12]
    copies = fetch(list(zip(inputs, loaded)), sems)
    for copy in copies:
        copy.wait()
    values, basis, transfer, far_plan, near_plan = loaded
    lift_tiles(cut(values), basis, transfer, own, up)
    far, near = far_plan[0, 0:1, :], near_plan[0, 0:1, :]
    blank = jnp.zeros((1, 128 - far.shape[1] - near.shape[1]), jnp.int32)
    row = jnp.concatenate([far, near, blank], axis=1).astype(F32)
    rows = jnp.broadcast_to(row, (up.shape[1] - 64, 128)).astype(BF16)
    for c in range(up.shape[0]):
        up[c, 64:, :] = rows


def turn_tables(sources, table):
    row = 0
    for ref in sources:
        for i in range(ref.shape[0]):
            tile = ref[i]
            table[0, row] = tile
            table[1, row] = beside(tile[:, 64:], tile[:, :64])
            row += 1


def at_left(table, base, leaf):
    return table[leaf % 2, base + leaf // 2]


def at_right(table, base, leaf):
    return table[1 - leaf % 2, base + leaf // 2]


def pair_of(table, base, first, second, left):
    return jnp.where(left, at_left(table, base, first), at_right(table, base, second))


def left_mask():
    return lax.broadcasted_iota(jnp.int32, (64, 128), 1) < 64


def mate_offset(core):
    return jnp.where(core == 0, HOPS, HOPS - 1)


def pack_kernel(place_ref, asks, mate_asks, far_plan, near_plan, own, mate, *refs):
    outs, beyond, table = refs[:REACH], refs[REACH], refs[REACH + 1]
    core, chip = place_ref[0], place_ref[1]
    chips = asks.shape[0]
    turn_tables((own, mate), table)
    left = left_mask()
    half = own.shape[0]
    order = mate_offset(core)
    for i in range(PAIR_TILES):
        if i < FAR_TILES:
            plan, at, base = far_plan, order * CAP0 + 2 * i, half
        else:
            plan, at, base = near_plan, order * CAPN + 2 * (i - FAR_TILES), half + half // 2
        first = jnp.maximum(plan[0, 0, at], 0)
        second = jnp.maximum(plan[0, 0, at + 1], 0)
        beyond[i] = pair_of(table, base, first, second, left)
    for step in range(REACH):
        toward = jnp.where(core == 0, -2 * (step + 1), 2 * (step + 1))
        asker = jnp.clip(chip - toward // 2, 0, chips - 1)
        for place, (other_target, other_source) in enumerate(PAIRS[step]):
            target = jnp.where(core == other_target, 0, 1)
            source = jnp.where(core == other_source, 0, 1)
            order = offset_index(toward + source - target)
            asked = mate_asks if other_target else asks
            for i in range(PAIR_TILES):
                if i < FAR_TILES:
                    at = order * CAP0 + 2 * i
                    base = other_source * half
                else:
                    at = OFFSETS * CAP0 + order * CAPN + 2 * (i - FAR_TILES)
                    base = other_source * half + half // 2
                first = jnp.maximum(asked[asker, at], 0)
                second = jnp.maximum(asked[asker, at + 1], 0)
                outs[step][place * PAIR_TILES + i] = pair_of(table, base, first, second, left)


def fetch(pairs, sems):
    copies = []
    for i, (source, target) in enumerate(pairs):
        copy = pltpu.make_async_copy(source, target, sems.at[i])
        copy.start()
        copies.append(copy)
    return copies


CHUNKS = 4


def local_body(
    place_ref, far_list, near_list, far_plan, near_plan, own_in, beyond_in, far_in, near_in, out,
    table, own, beyond, far_blocks, near_blocks, sems, far_remote, near_remote, further, lean=False
):
    core = place_ref[0]
    leaves = far_blocks.shape[0]
    step = leaves // CHUNKS
    pairs = [(own_in, own)]
    for c in range(CHUNKS):
        rows = pl.ds(c * step, step)
        pairs += [(far_in.at[rows], far_blocks.at[rows]), (near_in.at[rows], near_blocks.at[rows])]
    order = mate_offset(core)
    if lean:
        (far_from, far_to), (near_from, near_to) = further
        further = [
            (far_from.at[pl.ds(order * CAP0, CAP0)], far_to),
            (near_from.at[pl.ds(order * CAPN, CAPN)], near_to),
        ]
    copies = fetch(pairs + [(beyond_in, beyond)] + further, sems)
    copies[0].wait()
    turn_tables((own,), table)
    left = left_mask()
    half = own.shape[0]
    for leaf in range(leaves):
        if leaf % step == 0:
            c = leaf // step
            copies[1 + 2 * c].wait()
            copies[2 + 2 * c].wait()
        sums = []
        for listed, blocks, base in (
            (far_list, far_blocks, 0),
            (near_list, near_blocks, half // 2),
        ):
            xs, ws = [], []
            for k in range(0, blocks.shape[1], 2):
                xs.append(pair_of(table, base, listed[k, leaf], listed[k + 1, leaf], left))
                ws.append(beside(blocks[leaf, k], blocks[leaf, k + 1]))
            total = nt(jnp.concatenate(xs, axis=1), jnp.concatenate(ws, axis=1))
            sums.append(beside(total, jnp.zeros_like(total)))
        out[0, leaf], out[1, leaf] = sums
    for copy in copies[1 + 2 * CHUNKS :]:
        copy.wait()
    out[:, leaves] = jnp.zeros((2, 64, 128), F32)
    for i in range(PAIR_TILES):
        if i < FAR_TILES:
            kind, plan, blocks, at, cap = 0, far_plan, far_remote, 2 * i, CAP0
        else:
            kind, plan, blocks, at, cap = 1, near_plan, near_remote, 2 * (i - FAR_TILES), CAPN
        slot = order * cap + at
        first = at if lean else slot
        y = nt(beyond[i], diagonal(blocks[first], blocks[first + 1]))
        t0, t1 = plan[0, 1, slot], plan[0, 1, slot + 1]
        t0, t1 = jnp.where(t0 < 0, leaves, t0), jnp.where(t1 < 0, leaves, t1)
        out[kind, t0, :, 0:64] = out[kind, t0, :, 0:64] + y[:, 0:64]
        out[kind, t1, :, 64:128] = out[kind, t1, :, 64:128] + y[:, 64:128]


def local_kernel(*refs):
    ins, statics, out, held, scratch = refs[:9], refs[9:14], refs[14], refs[15:20], refs[20:]
    local_body(*ins, out, *scratch, held[0], held[1], list(zip(statics, held)))


def lean_local_kernel(*refs):
    ins, remote, out, scratch, held = refs[:9], refs[9:11], refs[11], refs[12:18], refs[18:]
    local_body(*ins, out, *scratch, *held, list(zip(remote, held)), lean=True)


def diagonal(b0, b1):
    zero = jnp.zeros_like(b0)
    return jnp.concatenate([beside(b0, zero), beside(zero, b1)], axis=0)


def add_slots(core, side, tile_at, far_plan, near_plan, far_remote, near_remote, acc):
    leaves = acc.shape[1] - 1
    for step in range(REACH):
        for other_target, other in PAIRS[step]:
            if other_target != side:
                continue
            sender = jnp.where(core == side, 0, 1)
            source = jnp.where(sender == other, 0, 1)
            away = jnp.where(sender == 0, -2 * (step + 1), 2 * (step + 1))
            order = offset_index(away + source - core)
            for i in range(PAIR_TILES):
                if i < FAR_TILES:
                    kind, plan, blocks = 0, far_plan, far_remote
                    slot = order * CAP0 + 2 * i
                else:
                    kind, plan, blocks = 1, near_plan, near_remote
                    slot = order * CAPN + 2 * (i - FAR_TILES)
                y = nt(tile_at(step, other, i), diagonal(blocks[slot], blocks[slot + 1]))
                t0, t1 = plan[0, 1, slot], plan[0, 1, slot + 1]
                t0, t1 = jnp.where(t0 < 0, leaves, t0), jnp.where(t1 < 0, leaves, t1)
                acc[kind, t0, :, 0:64] = acc[kind, t0, :, 0:64] + y[:, 0:64]
                acc[kind, t1, :, 64:128] = acc[kind, t1, :, 64:128] + y[:, 64:128]


def add_parents(core, side, chips, tile_at, parent_plan, parent_remote, total):
    left = left_mask()
    member = jnp.where(core == side, 0, 1)

    def one_chip(chip):
        tile = tile_at(chip)
        turned = beside(tile[:, 64:], tile[:, :64])
        slot = (2 * chip + member) * 2
        s0, s1 = parent_plan[0, 0, slot], parent_plan[0, 0, slot + 1]
        t0, t1 = parent_plan[0, 1, slot], parent_plan[0, 1, slot + 1]
        x0 = jnp.where(s0 > 0, turned, tile)
        x1 = jnp.where(s1 == 0, turned, tile)
        zero = jnp.zeros_like(tile)
        rows = []
        for p in range(2):
            x = jnp.where(left, jnp.where(t0 == p, x0, zero), jnp.where(t1 == p, x1, zero))
            rows.append(x)
        return jnp.concatenate(rows, axis=0), beside(parent_remote[slot], parent_remote[slot + 1])

    def two_chips(index, total):
        (x0, w0), (x1, w1) = one_chip(2 * index), one_chip(2 * index + 1)
        return total + nt(beside(x0, x1), beside(w0, w1))

    if chips % 2:
        total = total + nt(*one_chip(chips - 1))
    if chips <= 8:
        for index in range(chips // 2):
            total = two_chips(index, total)
        return total
    return lax.fori_loop(0, chips // 2, two_chips, total)


def arrived_kernel(*refs):
    place_ref, far_plan, near_plan, parent_plan = refs[:4]
    arrived = refs[4 : 4 + REACH]
    parents, _, far_remote, near_remote, parent_remote, acc, total = refs[4 + REACH :]
    core = place_ref[0]
    add_slots(
        core, 0, lambda step, other, i: arrived[step][other * PAIR_TILES + i],
        far_plan, near_plan, far_remote, near_remote, acc,
    )
    total[...] = add_parents(
        core, 0, parents.shape[0], lambda chip: parents[chip, 0:64, :],
        parent_plan, parent_remote, jnp.zeros((128, 64), F32),
    )


def swapped_body(
    place_ref, far_plan, near_plan, parent_plan, swapped, _, total, far_remote, near_remote,
    parent_remote, basis, transfer, acc
):
    core = place_ref[0]
    leaves = basis.shape[0]
    starts, rows = [], 0
    for pairs in PAIRS:
        starts.append(rows)
        rows += PAIR_TILES * (len(pairs) - 2)

    def tile_at(step, other, i):
        order = [o for t, o in PAIRS[step] if t == 1].index(other)
        return swapped[starts[step] + order * PAIR_TILES + i]

    add_slots(core, 1, tile_at, far_plan, near_plan, far_remote, near_remote, acc)
    parent_sum = add_parents(
        core, 1, swapped.shape[0] - rows, lambda chip: swapped[rows + chip],
        parent_plan, parent_remote, total[...],
    ).astype(BF16)
    left = left_mask()

    def leaf_pair(kind, i):
        a, b = acc[kind, 2 * i], acc[kind, 2 * i + 1]
        crossed = jnp.where(left, b, a)
        return jnp.where(left, a, b) + beside(crossed[:, 64:], crossed[:, :64])

    tiles = []
    for i in range(leaves // 2):
        p = 2 * i // FAN
        both = jnp.concatenate([transfer[2 * i], transfer[2 * i + 1]], axis=0)
        down = nt(parent_sum[64 * p : 64 * (p + 1)], both)
        summed = (leaf_pair(0, i) + down).astype(BF16)
        y = nt(summed, diagonal(basis[2 * i], basis[2 * i + 1])) + leaf_pair(1, i)
        tiles.append(y.astype(BF16))
    return tiles


def middle_kernel(*refs):
    inputs, (acc, out, own, up) = refs[:-4], refs[-4:]
    basis, transfer = inputs[-2:]
    tiles = swapped_body(*inputs, acc)
    for i, tile in enumerate(tiles):
        out[:, 128 * i : 128 * (i + 1)] = tile
    lift_tiles(tiles, basis, transfer, own, up)


def last_kernel(*refs):
    inputs, (acc, out) = refs[:-2], refs[-2:]
    for i, tile in enumerate(swapped_body(*inputs, acc)):
        out[:, 128 * i : 128 * (i + 1)] = tile


def call(kernel, kinds, outs, scratch, args, flops, limit=24, aliases=None):
    size = sum(a.size * a.dtype.itemsize for a in args)
    return pl.pallas_call(
        kernel,
        out_shape=outs,
        in_specs=[SPECS[k] for k in kinds],
        out_specs=jax.tree.map(lambda _: VMEM, outs),
        scratch_shapes=scratch,
        input_output_aliases=aliases or {},
        compiler_params=pltpu.CompilerParams(vmem_limit_bytes=limit * MIB),
        cost_estimate=pl.CostEstimate(flops=int(flops), bytes_accessed=size, transcendentals=0),
    )(*args)


def on_device(
    values,
    basis,
    transfer,
    near_list,
    near_blocks,
    far_list,
    far_blocks,
    near_plan,
    near_remote,
    far_plan,
    far_remote,
    parent_plan,
    parent_remote,
):
    devices = lax.axis_size("clu")
    chips = devices // 2
    leaves = basis.shape[0]
    at = lax.axis_index("clu").astype(jnp.int32)
    place = jnp.stack([at & 1, at >> 1])
    near_remote, far_remote, parent_remote = near_remote[0], far_remote[0], parent_remote[0]
    far_remote = with_layout_constraint(far_remote, Layout((0, 1, 2)))
    far_list, near_list = far_list.T, near_list.T
    same_core = [[2 * c + k for c in range(chips)] for k in range(2)]

    shape = jax.ShapeDtypeStruct
    dma = pltpu.SemaphoreType.DMA
    own_shape = shape((leaves, 64, 128), BF16)
    beyond_shape = shape((PAIR_TILES, 64, 128), BF16)
    out_shape = shape((64, values.shape[0]), BF16)
    sums_shape = shape((2, leaves + 1, 64, 128), F32)
    statics = (far_remote, near_remote, parent_remote, basis, transfer)
    held_shapes = [pltpu.VMEM(x.shape, x.dtype) for x in statics]
    table_scratch = [pltpu.VMEM((2, 2 * leaves, 64, 128), BF16)]
    local_scratch = [
        pltpu.VMEM((2, leaves, 64, 128), BF16),
        pltpu.VMEM(own_shape.shape, BF16),
        pltpu.VMEM(beyond_shape.shape, BF16),
        pltpu.VMEM(far_blocks.shape, BF16),
        pltpu.VMEM(near_blocks.shape, BF16),
    ]
    messages = [shape((PAIR_TILES * len(p), 64, 128), BF16) for p in PAIRS]

    def crosswise(x):
        return lax.ppermute(x, "clu", mates(devices))

    def exchange(own, up, asks, last):
        nonlocal far_remote, statics
        parents = lax.all_to_all(up, "clu", 0, 0, tiled=True, axis_index_groups=same_core)
        mate = crosswise(own)
        if asks is None:
            parents, far_remote = lax.optimization_barrier((parents, far_remote))
            statics = (far_remote, *statics[1:])
            asks = parents[:, 64, :].astype(jnp.int32)
            asks = (asks, crosswise(asks))
        *packed, beyond = call(
            pack_kernel, "sssssvv", [*messages, beyond_shape], table_scratch,
            (place, *asks, far_plan, near_plan, own, mate), 2e9,
        )
        arrived = [
            lax.ppermute(m, "clu", outward(devices, d + 1)) for d, m in enumerate(packed)
        ]
        local = (place, far_list, near_list, far_plan, near_plan, own, beyond, far_blocks,
                 near_blocks)
        if last:
            held = statics
            sums = call(
                lean_local_kernel, "sssssaahhhh", sums_shape,
                local_scratch + [dma((4 + 2 * CHUNKS,))]
                + [pltpu.VMEM((n, 64, 64), BF16) for n in (CAP0, CAPN)],
                (*local, far_remote, near_remote), 6e9, 12,
            )
        else:
            sums, *held = call(
                local_kernel, "sssssaahh" + "h" * len(statics), [sums_shape, *held_shapes],
                local_scratch + [dma((2 + 2 * CHUNKS + len(statics),))], (*local, *statics), 7e9,
            )
        arrived, parents, sums = lax.optimization_barrier((arrived, parents, sums))
        swapped = jnp.concatenate([m[MINE:] for m in arrived] + [parents[:, :64]])
        swapped = crosswise(swapped)
        plans = (place, far_plan, near_plan, parent_plan)
        sums, total = call(
            arrived_kernel, "ssss" + "v" * (REACH + 5), [sums_shape, shape((128, 64), F32)], [],
            (*plans, *arrived, parents, sums, *held[:3]), 2e9, 16, {4 + REACH + 1: 0},
        )
        return (*plans, swapped, sums, total, *held), asks

    kinds = "ssss" + "v" * 8
    lifted = (values.T, basis, transfer, far_plan, near_plan)
    own, up = call(
        lift_kernel, "hhhhh", [own_shape, shape((chips, 80, 128), BF16)],
        [pltpu.VMEM(x.shape, x.dtype) for x in lifted] + [dma((len(lifted),))], lifted, 1e9,
        60,
    )
    inputs, asks = exchange(own, up, None, False)
    _, first, own, up = call(
        middle_kernel, kinds, [sums_shape, out_shape, own_shape, shape((chips, 64, 128), BF16)],
        [], inputs, 3e9, 16, {5: 0},
    )
    inputs, _ = exchange(own, up, asks, True)
    _, second = call(
        last_kernel, kinds, [sums_shape, out_shape], [], inputs, 2e9, 16, {5: 0}
    )
    return first.T, second.T


def solution(mesh):
    return jax.shard_map(
        on_device,
        mesh=mesh,
        in_specs=(
            P(("groups", "clu"), None),
            P(("groups", "clu"), None, None),
            P(("groups", "clu"), None, None),
            P(("groups", "clu"), None),
            P(("groups", "clu"), None, None, None),
            P(("groups", "clu"), None),
            P(("groups", "clu"), None, None, None),
            P(("groups", "clu"), None, None),
            P(("groups", "clu"), None, None, None),
            P(("groups", "clu"), None, None),
            P(("groups", "clu"), None, None, None),
            P(("groups", "clu"), None, None),
            P(("groups", "clu"), None, None, None),
        ),
        out_specs=(P(("groups", "clu"), None), P(("groups", "clu"), None)),
        check_vma=False,
    )
```

```python
import jax
import jax.numpy as jnp
from jax import lax
from jax.experimental.layout import Layout, with_layout_constraint
from jax.experimental import pallas as pl
from jax.experimental.pallas import tpu as pltpu
from jax.sharding import PartitionSpec as P


HOPS = 6
CAP0 = 6
CAPN = 2
FAN = 8
REACH = (HOPS + 1) // 2
OFFSETS = 2 * HOPS
FAR_TILES = CAP0 // 2
PAIR_TILES = (CAP0 + CAPN) // 2
F32 = jnp.float32
BF16 = jnp.bfloat16
VMEM = pl.BlockSpec(memory_space=pltpu.VMEM)
SMEM = pl.BlockSpec(memory_space=pltpu.SMEM)
ANY = pl.BlockSpec(memory_space=pl.ANY)
HBM = pl.BlockSpec(memory_space=pltpu.HBM)
MIB = 1024 * 1024
SPECS = {"s": SMEM, "v": VMEM, "a": ANY, "h": HBM}
PAIRS = [[(0, 0), (0, 1), (1, 0), (1, 1)]] * (REACH - 1) + [[(0, 0), (0, 1), (1, 1)]]
MINE = 2 * PAIR_TILES


def nn(a, b):
    return jnp.dot(a, b, preferred_element_type=F32)


def nt(a, b):
    return lax.dot_general(a, b, (((1,), (1,)), ((), ())), preferred_element_type=F32)


def beside(a, b):
    return jnp.concatenate([a, b], axis=1)


def outward(devices, by):
    chips = devices // 2
    up = [(2 * c, 2 * (c + by)) for c in range(chips) if c + by < chips]
    return up + [(2 * c + 1, 2 * (c - by) + 1) for c in range(chips) if c - by >= 0]


def mates(devices):
    return [(i, i ^ 1) for i in range(devices)]


def offset_index(off):
    where = off + HOPS - jnp.where(off > 0, 1, 0)
    return jnp.clip(where, 0, OFFSETS - 1)


def lift_tiles(tiles, basis, transfer, own, up, pending=()):
    count = len(tiles)
    sums, lifted = [], []
    width = basis.shape[1]
    for i, tile in enumerate(tiles):
        c0 = nn(tile[:, :width], basis[2 * i])
        c1 = nn(tile[:, width:], basis[2 * i + 1])
        coarse = beside(c0, c1).astype(BF16)
        own[i] = coarse
        own[count + i] = tile
        lifted.append(coarse)
    for copy in pending:
        copy.wait()
    for i, coarse in enumerate(lifted):
        part = nn(coarse[:, :width], transfer[2 * i]) + nn(coarse[:, width:], transfer[2 * i + 1])
        if i % (FAN // 2) == 0:
            sums.append(part)
        else:
            sums[-1] = sums[-1] + part
    parents = beside(*sums).astype(BF16)
    for c in range(up.shape[0]):
        up[c, 0:64, :] = parents


def cut(values):
    return [values[:, 128 * i : 128 * (i + 1)] for i in range(values.shape[1] // 128)]


def lift_kernel(*refs):
    inputs, (own, up), loaded, sems = refs[:5], refs[5:7], refs[7:12], refs[12]
    copies = fetch(list(zip(inputs, loaded)), sems)
    for copy in copies[:2]:
        copy.wait()
    values, basis, transfer, far_plan, near_plan = loaded
    lift_tiles(cut(values), basis, transfer, own, up, copies[2:])
    far, near = far_plan[0, 0:1, :], near_plan[0, 0:1, :]
    blank = jnp.zeros((1, 128 - far.shape[1] - near.shape[1]), jnp.int32)
    row = jnp.concatenate([far, near, blank], axis=1).astype(F32)
    rows = jnp.broadcast_to(row, (up.shape[1] - 64, 128)).astype(BF16)
    for c in range(up.shape[0]):
        up[c, 64:, :] = rows


def turn_tables(sources, table):
    row = 0
    for ref in sources:
        for i in range(ref.shape[0]):
            tile = ref[i]
            table[0, row] = tile
            table[1, row] = beside(tile[:, 64:], tile[:, :64])
            row += 1


def at_left(table, base, leaf):
    return table[leaf % 2, base + leaf // 2]


def at_right(table, base, leaf):
    return table[1 - leaf % 2, base + leaf // 2]


def pair_of(table, base, first, second, left):
    return jnp.where(left, at_left(table, base, first), at_right(table, base, second))


def left_mask():
    return lax.broadcasted_iota(jnp.int32, (64, 128), 1) < 64


def mate_offset(core):
    return jnp.where(core == 0, HOPS, HOPS - 1)


def pack_kernel(place_ref, asks, mate_asks, far_plan, near_plan, own, mate, *refs):
    outs, beyond, table = refs[:REACH], refs[REACH], refs[REACH + 1]
    core, chip = place_ref[0], place_ref[1]
    chips = asks.shape[0]
    turn_tables((own, mate), table)
    left = left_mask()
    half = own.shape[0]
    order = mate_offset(core)
    for i in range(PAIR_TILES):
        if i < FAR_TILES:
            plan, at, base = far_plan, order * CAP0 + 2 * i, half
        else:
            plan, at, base = near_plan, order * CAPN + 2 * (i - FAR_TILES), half + half // 2
        first = jnp.maximum(plan[0, 0, at], 0)
        second = jnp.maximum(plan[0, 0, at + 1], 0)
        beyond[i] = pair_of(table, base, first, second, left)
    for step in range(REACH):
        toward = jnp.where(core == 0, -2 * (step + 1), 2 * (step + 1))
        asker = jnp.clip(chip - toward // 2, 0, chips - 1)
        for place, (other_target, other_source) in enumerate(PAIRS[step]):
            target = jnp.where(core == other_target, 0, 1)
            source = jnp.where(core == other_source, 0, 1)
            order = offset_index(toward + source - target)
            asked = mate_asks if other_target else asks
            for i in range(PAIR_TILES):
                if i < FAR_TILES:
                    at = order * CAP0 + 2 * i
                    base = other_source * half
                else:
                    at = OFFSETS * CAP0 + order * CAPN + 2 * (i - FAR_TILES)
                    base = other_source * half + half // 2
                first = jnp.maximum(asked[asker, at], 0)
                second = jnp.maximum(asked[asker, at + 1], 0)
                outs[step][place * PAIR_TILES + i] = pair_of(table, base, first, second, left)


def fetch(pairs, sems):
    copies = []
    for i, (source, target) in enumerate(pairs):
        copy = pltpu.make_async_copy(source, target, sems.at[i])
        copy.start()
        copies.append(copy)
    return copies


CHUNKS = 4


def local_body(
    place_ref, far_list, near_list, far_plan, near_plan, own_in, beyond_in, far_in, near_in, out,
    table, own, beyond, far_blocks, near_blocks, sems, far_remote, near_remote, further, lean=False
):
    core = place_ref[0]
    leaves = far_blocks.shape[0]
    step = leaves // CHUNKS
    pairs = [(own_in, own)]
    for c in range(CHUNKS):
        rows = pl.ds(c * step, step)
        pairs += [(far_in.at[rows], far_blocks.at[rows]), (near_in.at[rows], near_blocks.at[rows])]
    order = mate_offset(core)
    if lean:
        (far_from, far_to), (near_from, near_to) = further
        further = [
            (far_from.at[pl.ds(order * CAP0, CAP0)], far_to),
            (near_from.at[pl.ds(order * CAPN, CAPN)], near_to),
        ]
    copies = fetch(pairs + [(beyond_in, beyond)] + further, sems)
    copies[0].wait()
    turn_tables((own,), table)
    left = left_mask()
    half = own.shape[0]
    for leaf in range(leaves):
        if leaf % step == 0:
            c = leaf // step
            copies[1 + 2 * c].wait()
            copies[2 + 2 * c].wait()
        sums = []
        for listed, blocks, base in (
            (far_list, far_blocks, 0),
            (near_list, near_blocks, half // 2),
        ):
            xs, ws = [], []
            for k in range(0, blocks.shape[1], 2):
                xs.append(pair_of(table, base, listed[k, leaf], listed[k + 1, leaf], left))
                ws.append(beside(blocks[leaf, k], blocks[leaf, k + 1]))
            total = nt(jnp.concatenate(xs, axis=1), jnp.concatenate(ws, axis=1))
            sums.append(beside(total, jnp.zeros_like(total)))
        out[0, leaf], out[1, leaf] = sums
    for copy in copies[1 + 2 * CHUNKS :]:
        copy.wait()
    out[:, leaves] = jnp.zeros((2, 64, 128), F32)
    for i in range(PAIR_TILES):
        if i < FAR_TILES:
            kind, plan, blocks, at, cap = 0, far_plan, far_remote, 2 * i, CAP0
        else:
            kind, plan, blocks, at, cap = 1, near_plan, near_remote, 2 * (i - FAR_TILES), CAPN
        slot = order * cap + at
        first = at if lean else slot
        y = nt(beyond[i], diagonal(blocks[first], blocks[first + 1]))
        t0, t1 = plan[0, 1, slot], plan[0, 1, slot + 1]
        t0, t1 = jnp.where(t0 < 0, leaves, t0), jnp.where(t1 < 0, leaves, t1)
        out[kind, t0, :, 0:64] = out[kind, t0, :, 0:64] + y[:, 0:64]
        out[kind, t1, :, 64:128] = out[kind, t1, :, 64:128] + y[:, 64:128]


def local_kernel(*refs):
    ins, statics, out, held, scratch = refs[:9], refs[9:14], refs[14], refs[15:20], refs[20:]
    local_body(*ins, out, *scratch, held[0], held[1], list(zip(statics, held)))


def lean_local_kernel(*refs):
    ins, remote, out, scratch, held = refs[:9], refs[9:11], refs[11], refs[12:18], refs[18:]
    local_body(*ins, out, *scratch, *held, list(zip(remote, held)), lean=True)


def diagonal(b0, b1):
    zero = jnp.zeros_like(b0)
    return jnp.concatenate([beside(b0, zero), beside(zero, b1)], axis=0)


def add_slots(core, side, tile_at, far_plan, near_plan, far_remote, near_remote, acc):
    leaves = acc.shape[1] - 1
    for step in range(REACH):
        for other_target, other in PAIRS[step]:
            if other_target != side:
                continue
            sender = jnp.where(core == side, 0, 1)
            source = jnp.where(sender == other, 0, 1)
            away = jnp.where(sender == 0, -2 * (step + 1), 2 * (step + 1))
            order = offset_index(away + source - core)
            for i in range(PAIR_TILES):
                if i < FAR_TILES:
                    kind, plan, blocks = 0, far_plan, far_remote
                    slot = order * CAP0 + 2 * i
                else:
                    kind, plan, blocks = 1, near_plan, near_remote
                    slot = order * CAPN + 2 * (i - FAR_TILES)
                y = nt(tile_at(step, other, i), diagonal(blocks[slot], blocks[slot + 1]))
                t0, t1 = plan[0, 1, slot], plan[0, 1, slot + 1]
                t0, t1 = jnp.where(t0 < 0, leaves, t0), jnp.where(t1 < 0, leaves, t1)
                acc[kind, t0, :, 0:64] = acc[kind, t0, :, 0:64] + y[:, 0:64]
                acc[kind, t1, :, 64:128] = acc[kind, t1, :, 64:128] + y[:, 64:128]


def add_parents(core, side, chips, tile_at, parent_plan, parent_remote, total):
    left = left_mask()
    member = jnp.where(core == side, 0, 1)

    def one_chip(chip):
        tile = tile_at(chip)
        turned = beside(tile[:, 64:], tile[:, :64])
        slot = (2 * chip + member) * 2
        s0, s1 = parent_plan[0, 0, slot], parent_plan[0, 0, slot + 1]
        t0, t1 = parent_plan[0, 1, slot], parent_plan[0, 1, slot + 1]
        x0 = jnp.where(s0 > 0, turned, tile)
        x1 = jnp.where(s1 == 0, turned, tile)
        zero = jnp.zeros_like(tile)
        rows = []
        for p in range(2):
            x = jnp.where(left, jnp.where(t0 == p, x0, zero), jnp.where(t1 == p, x1, zero))
            rows.append(x)
        return jnp.concatenate(rows, axis=0), beside(parent_remote[slot], parent_remote[slot + 1])

    def two_chips(index, total):
        (x0, w0), (x1, w1) = one_chip(2 * index), one_chip(2 * index + 1)
        return total + nt(beside(x0, x1), beside(w0, w1))

    if chips % 2:
        total = total + nt(*one_chip(chips - 1))
    if chips <= 8:
        for index in range(chips // 2):
            total = two_chips(index, total)
        return total
    return lax.fori_loop(0, chips // 2, two_chips, total)


def arrived_kernel(*refs):
    place_ref, far_plan, near_plan, parent_plan = refs[:4]
    arrived = refs[4 : 4 + REACH]
    parents, _, far_remote, near_remote, parent_remote, acc, total = refs[4 + REACH :]
    core = place_ref[0]
    add_slots(
        core, 0, lambda step, other, i: arrived[step][other * PAIR_TILES + i],
        far_plan, near_plan, far_remote, near_remote, acc,
    )
    total[...] = add_parents(
        core, 0, parents.shape[0], lambda chip: parents[chip, 0:64, :],
        parent_plan, parent_remote, jnp.zeros((128, 64), F32),
    )


def swapped_body(
    place_ref, far_plan, near_plan, parent_plan, swapped, _, total, far_remote, near_remote,
    parent_remote, basis, transfer, acc
):
    core = place_ref[0]
    leaves = basis.shape[0]
    starts, rows = [], 0
    for pairs in PAIRS:
        starts.append(rows)
        rows += PAIR_TILES * (len(pairs) - 2)

    def tile_at(step, other, i):
        order = [o for t, o in PAIRS[step] if t == 1].index(other)
        return swapped[starts[step] + order * PAIR_TILES + i]

    add_slots(core, 1, tile_at, far_plan, near_plan, far_remote, near_remote, acc)
    parent_sum = add_parents(
        core, 1, swapped.shape[0] - rows, lambda chip: swapped[rows + chip],
        parent_plan, parent_remote, total[...],
    ).astype(BF16)
    left = left_mask()

    def leaf_pair(kind, i):
        a, b = acc[kind, 2 * i], acc[kind, 2 * i + 1]
        crossed = jnp.where(left, b, a)
        return jnp.where(left, a, b) + beside(crossed[:, 64:], crossed[:, :64])

    tiles = []
    for i in range(leaves // 2):
        p = 2 * i // FAN
        both = jnp.concatenate([transfer[2 * i], transfer[2 * i + 1]], axis=0)
        down = nt(parent_sum[64 * p : 64 * (p + 1)], both)
        summed = (leaf_pair(0, i) + down).astype(BF16)
        y = nt(summed, diagonal(basis[2 * i], basis[2 * i + 1])) + leaf_pair(1, i)
        tiles.append(y.astype(BF16))
    return tiles


def middle_kernel(*refs):
    inputs, (acc, out, own, up) = refs[:-4], refs[-4:]
    basis, transfer = inputs[-2:]
    tiles = swapped_body(*inputs, acc)
    for i, tile in enumerate(tiles):
        out[:, 128 * i : 128 * (i + 1)] = tile
    lift_tiles(tiles, basis, transfer, own, up)


def last_kernel(*refs):
    inputs, (acc, out) = refs[:-2], refs[-2:]
    for i, tile in enumerate(swapped_body(*inputs, acc)):
        out[:, 128 * i : 128 * (i + 1)] = tile


def call(kernel, kinds, outs, scratch, args, flops, limit=24, aliases=None):
    size = sum(a.size * a.dtype.itemsize for a in args)
    return pl.pallas_call(
        kernel,
        out_shape=outs,
        in_specs=[SPECS[k] for k in kinds],
        out_specs=jax.tree.map(lambda _: VMEM, outs),
        scratch_shapes=scratch,
        input_output_aliases=aliases or {},
        compiler_params=pltpu.CompilerParams(vmem_limit_bytes=limit * MIB),
        cost_estimate=pl.CostEstimate(flops=int(flops), bytes_accessed=size, transcendentals=0),
    )(*args)


def on_device(
    values,
    basis,
    transfer,
    near_list,
    near_blocks,
    far_list,
    far_blocks,
    near_plan,
    near_remote,
    far_plan,
    far_remote,
    parent_plan,
    parent_remote,
):
    devices = lax.axis_size("clu")
    chips = devices // 2
    leaves = basis.shape[0]
    at = lax.axis_index("clu").astype(jnp.int32)
    place = jnp.stack([at & 1, at >> 1])
    near_remote, far_remote, parent_remote = near_remote[0], far_remote[0], parent_remote[0]
    far_remote = with_layout_constraint(far_remote, Layout((0, 1, 2)))
    far_list, near_list = far_list.T, near_list.T
    same_core = [[2 * c + k for c in range(chips)] for k in range(2)]

    shape = jax.ShapeDtypeStruct
    dma = pltpu.SemaphoreType.DMA
    own_shape = shape((leaves, 64, 128), BF16)
    beyond_shape = shape((PAIR_TILES, 64, 128), BF16)
    out_shape = shape((64, values.shape[0]), BF16)
    sums_shape = shape((2, leaves + 1, 64, 128), F32)
    statics = (far_remote, near_remote, parent_remote, basis, transfer)
    held_shapes = [pltpu.VMEM(x.shape, x.dtype) for x in statics]
    table_scratch = [pltpu.VMEM((2, 2 * leaves, 64, 128), BF16)]
    local_scratch = [
        pltpu.VMEM((2, leaves, 64, 128), BF16),
        pltpu.VMEM(own_shape.shape, BF16),
        pltpu.VMEM(beyond_shape.shape, BF16),
        pltpu.VMEM(far_blocks.shape, BF16),
        pltpu.VMEM(near_blocks.shape, BF16),
    ]
    messages = [shape((PAIR_TILES * len(p), 64, 128), BF16) for p in PAIRS]

    def crosswise(x):
        return lax.ppermute(x, "clu", mates(devices))

    def exchange(own, up, asks, last):
        nonlocal far_remote, statics
        parents = lax.all_to_all(up, "clu", 0, 0, tiled=True, axis_index_groups=same_core)
        mate = crosswise(own)
        if asks is None:
            parents, far_remote = lax.optimization_barrier((parents, far_remote))
            statics = (far_remote, *statics[1:])
            asks = parents[:, 64, :].astype(jnp.int32)
            asks = (asks, crosswise(asks))
        *packed, beyond = call(
            pack_kernel, "sssssvv", [*messages, beyond_shape], table_scratch,
            (place, *asks, far_plan, near_plan, own, mate), 2e9,
        )
        arrived = [
            lax.ppermute(m, "clu", outward(devices, d + 1)) for d, m in enumerate(packed)
        ]
        local = (place, far_list, near_list, far_plan, near_plan, own, beyond, far_blocks,
                 near_blocks)
        if last:
            held = statics
            sums = call(
                lean_local_kernel, "sssssaahhhh", sums_shape,
                local_scratch + [dma((4 + 2 * CHUNKS,))]
                + [pltpu.VMEM((n, 64, 64), BF16) for n in (CAP0, CAPN)],
                (*local, far_remote, near_remote), 6e9, 12,
            )
        else:
            sums, *held = call(
                local_kernel, "sssssaahh" + "h" * len(statics), [sums_shape, *held_shapes],
                local_scratch + [dma((2 + 2 * CHUNKS + len(statics),))], (*local, *statics), 7e9,
            )
        arrived, parents, sums = lax.optimization_barrier((arrived, parents, sums))
        swapped = jnp.concatenate([m[MINE:] for m in arrived] + [parents[:, :64]])
        swapped = crosswise(swapped)
        plans = (place, far_plan, near_plan, parent_plan)
        sums, total = call(
            arrived_kernel, "ssss" + "v" * (REACH + 5), [sums_shape, shape((128, 64), F32)], [],
            (*plans, *arrived, parents, sums, *held[:3]), 2e9, 16, {4 + REACH + 1: 0},
        )
        return (*plans, swapped, sums, total, *held), asks

    kinds = "ssss" + "v" * 8
    lifted = (values.T, basis, transfer, far_plan, near_plan)
    own, up = call(
        lift_kernel, "hhhhh", [own_shape, shape((chips, 80, 128), BF16)],
        [pltpu.VMEM(x.shape, x.dtype) for x in lifted] + [dma((len(lifted),))], lifted, 1e9,
        60,
    )
    inputs, asks = exchange(own, up, None, False)
    _, first, own, up = call(
        middle_kernel, kinds, [sums_shape, out_shape, own_shape, shape((chips, 64, 128), BF16)],
        [], inputs, 3e9, 16, {5: 0},
    )
    inputs, _ = exchange(own, up, asks, True)
    _, second = call(
        last_kernel, kinds, [sums_shape, out_shape], [], inputs, 2e9, 16, {5: 0}
    )
    return first.T, second.T


def solution(mesh):
    return jax.shard_map(
        on_device,
        mesh=mesh,
        in_specs=(
            P(("groups", "clu"), None),
            P(("groups", "clu"), None, None),
            P(("groups", "clu"), None, None),
            P(("groups", "clu"), None),
            P(("groups", "clu"), None, None, None),
            P(("groups", "clu"), None),
            P(("groups", "clu"), None, None, None),
            P(("groups", "clu"), None, None),
            P(("groups", "clu"), None, None, None),
            P(("groups", "clu"), None, None),
            P(("groups", "clu"), None, None, None),
            P(("groups", "clu"), None, None),
            P(("groups", "clu"), None, None, None),
        ),
        out_specs=(P(("groups", "clu"), None), P(("groups", "clu"), None)),
        check_vma=False,
    )
```
